32 devices in a mesh: row: 4 (over y, x), col: 8 (over z, core).
Axes of the slice: x: 2, y: 2, z: 4, core: 2. Of those that a mesh axis runs over, the one named last changes fastest.
Arguments:
- pair_state: bfloat16 [192, 192, 128], P(('row', 'col')), may hold values from -6 to 6
- single_rep: bfloat16 [16, 192, 768], P(None, ('row', 'col')), may hold values from -64 to 64
- token_mask: int32 [192], replicated, may hold values 0 or 1
- chain_ids: int32 [192], replicated, may hold values from 0 to 3, never falling along the last dimension, each value on 1 to 96 neighbouring positions
- pair_gain: float32 [128], replicated, may hold values from 0.1 to 1.9
- mix_gain: float32 [128], replicated, may hold values from 0.1 to 1.9
- left_weight: bfloat16 [128, 256], replicated, may hold values from -0.5 to 0.5
- right_weight: bfloat16 [128, 256], replicated, may hold values from -0.5 to 0.5
- gate_weight: bfloat16 [128, 128], replicated, may hold values from -0.5 to 0.5
- out_weight: bfloat16 [128, 128], replicated, may hold values from -0.5 to 0.5
- bias_weight: bfloat16 [128, 16], replicated, may hold values from -1.5 to 1.5
- token_weight: bfloat16 [768, 2304], replicated, may hold values from -0.21875 to 0.21875
- merge_weight: bfloat16 [768, 768], replicated, may hold values from -0.625 to 0.625
Outputs:
- pair_tiles: bfloat16 [192, 4, 8, 6, 128], P('row', None, 'col')
- attention_out: bfloat16 [16, 192, 768], P(None, ('row', 'col'))
The draws below stay inside these ranges and needn't reach their ends.
Inputs may be any that keep to these rules, and one draw needn't show every extreme that they name: chain_ids never falls along the tokens; a chain holds 1 to 96 tokens.
All inputs are finite; a program needn't handle non-finite values.
Results may differ from the reference program's by a relative error of at most 0.034.
Values may be sent and summed in bfloat16 or wider, within the bound.
No kernel may reach another device: no remote copies, remote signals or barrier semaphores. Data moves between devices by JAX's collectives and lax.ppermute only.
A program may use at most 256 MiB of HBM per device.

```python
import math
import jax
import jax.numpy as jnp
import numpy as np
from jax import lax

C = 128
HEADS = 16
HEAD_DIM = 48
D = 768
SAMPLES = 16
TOK_FLAT = 6
TOKENS = 192
N_ROW = 4
N_COL = 8


def draw_single_rep(key, part):
    full_shape = (SAMPLES, TOKENS, D)
    base_key = jax.random.fold_in(jax.random.fold_in(key, 11), 0)
    return jnp.clip(jax.random.normal(base_key, full_shape, jnp.float32), -6.0, 6.0).astype(jnp.bfloat16)


def with_ends(values, rng, smallest, top_value):
    extent = values.shape
    index_at = [jax.random.randint(jax.random.fold_in(rng, axis), (), 0, extent[axis]) for axis in range(len(extent))]
    values = values.at[tuple(index_at)].set(smallest)
    longest = extent.index(max(extent))
    index_at[longest] = (index_at[longest] + 1) % extent[longest]
    return values.at[tuple(index_at)].set(top_value)


def steps_of(rng, dims, shards, low, largest):
    level, own = 1.0, jax.random.fold_in(rng, 6)
    for axis_at, blocks in shards:
        steps = jnp.exp(jax.random.uniform(jax.random.fold_in(own, axis_at), (blocks,), jnp.float32, low / len(shards), largest / len(shards)))
        level = level * jnp.repeat(steps, dims[axis_at] // blocks).reshape([-1 if axis == axis_at else 1 for axis in range(len(dims))])
    return level


def split_up(number_of, total, limit, skew):
    weights = [(1 << 20) // math.isqrt(standing ** skew) + 1 for standing in range(2, number_of + 1)]
    rest, counts = total - limit - (number_of - 1), [1] * (number_of - 1)
    while rest > 0:
        candidates = [i for i in range(number_of - 1) if counts[i] < limit]
        whole, remaining = sum([weights[i] for i in candidates]), rest
        for i in candidates:
            extra = min(limit - counts[i], max(1, remaining * weights[i] // whole), rest)
            counts[i] = counts[i] + extra
            rest = rest - extra
    return np.array([limit] + counts)


def uneven_parts(rng, number_of, total, most, slope):
    if number_of == 2:
        one = jax.random.randint(rng, (), max(1, total - most), min(most, total - 1) + 1)
        return jnp.stack([one, total - one])
    tallies = jnp.asarray(split_up(number_of, total, most, slope), jnp.int32)
    pairs = (number_of - 1) // 2
    giver, sink = tallies[1:1 + 2 * pairs:2], tallies[2:2 + 2 * pairs:2]
    slack = jnp.minimum(giver - 1, most - sink)
    moved = jax.random.randint(jax.random.fold_in(rng, 1), (pairs,), 0, 1 << 20) % (slack + 1)
    tallies = tallies.at[1:1 + 2 * pairs:2].set(giver - moved).at[2:2 + 2 * pairs:2].set(sink + moved)
    return tallies[jax.random.permutation(jax.random.fold_in(rng, 2), number_of)]


def gaussian(rng, shape, deviation, limit, cuts=(), kind=jnp.bfloat16):
    values = jax.random.normal(rng, shape, jnp.float32) * deviation
    if len(cuts) > 0:
        values = steps_of(rng, shape, cuts, -0.22, 0.18) * values
    return jnp.clip(values, min=-limit, max=limit).astype(kind)


def setup_inputs(seed: int = 0) -> dict:
    key_of = jax.random.split(jax.random.key(seed), 14)
    pair_state = gaussian(key_of[0], (TOKENS, TOKENS, C), 1.0, 6.0, ((0, 32),))
    single_rep = draw_single_rep(jax.random.fold_in(key_of[13], 71), 0)
    token_mask = with_ends((jax.random.randint(key_of[2], (TOKENS,), 0, 8) < 7).astype(jnp.int32), jax.random.fold_in(key_of[2], 1), 0, 1)
    chain_ids = jnp.searchsorted(jnp.cumsum(uneven_parts(key_of[3], 4, TOKENS, TOKENS // 2, 0)), jnp.arange(TOKENS), side="right").astype(jnp.int32)
    pair_gain = jnp.clip(1.0 + 0.18 * jax.random.normal(key_of[4], (C,), jnp.float32), 0.1, 1.9)
    mix_gain = jnp.clip(1.0 + 0.18 * jax.random.normal(key_of[5], (C,), jnp.float32), 0.1, 1.9)
    left_weight = gaussian(key_of[6], (C, 2 * C), C ** -0.5, 0.5)
    right_weight = gaussian(key_of[7], (C, 2 * C), C ** -0.5, 0.5)
    gate_weight = gaussian(key_of[8], (C, C), C ** -0.5, 0.5)
    out_weight = gaussian(key_of[9], (C, C), C ** -0.5, 0.5)
    bias_weight = gaussian(key_of[10], (C, HEADS), 0.25, 1.5)
    token_weight = gaussian(key_of[11], (D, 3 * D), D ** -0.5, 0.21875)
    merge_weight = gaussian(key_of[12], (D, D), (D // 8) ** -0.5, 0.625)
    return {"pair_state": pair_state, "single_rep": single_rep, "token_mask": token_mask, "chain_ids": chain_ids, "pair_gain": pair_gain, "mix_gain": mix_gain, "left_weight": left_weight, "right_weight": right_weight, "gate_weight": gate_weight, "out_weight": out_weight, "bias_weight": bias_weight, "token_weight": token_weight, "merge_weight": merge_weight}


epsilon = 1e-05

def normalize(values, norm_gain):
    floats = values.astype(jnp.float32)
    centered = floats - lax.optimization_barrier(jnp.mean(floats, axis=-1, keepdims=True))
    variance = lax.optimization_barrier(jnp.mean(centered * centered, axis=-1, keepdims=True))
    scaled = centered * lax.rsqrt(variance + epsilon)
    if norm_gain is None:
        return scaled
    return scaled * norm_gain

def gated_branch(normed, weight, pair_mask):
    half_width = weight.shape[0]
    hidden = jnp.dot(normed.reshape(-1, half_width), weight, preferred_element_type=jnp.float32)
    hidden = hidden.reshape(normed.shape[0], normed.shape[1], 2 * half_width)
    return (jax.nn.sigmoid(hidden[..., :half_width]) * hidden[..., half_width:] * pair_mask[..., None]).astype(jnp.bfloat16)

def project_pairs(normed, weight):
    result = jnp.dot(normed.reshape(-1, normed.shape[-1]), weight, preferred_element_type=jnp.float32)
    return result.reshape(normed.shape[0], normed.shape[1], weight.shape[1])

def reference(pair_state, single_rep, token_mask, chain_ids, pair_gain, mix_gain, left_weight, right_weight, gate_weight, out_weight, bias_weight, token_weight, merge_weight):
    valid_all = (token_mask == 1).astype(jnp.float32)
    pair_mask = valid_all[:, None] * valid_all[None, :]
    normed = normalize(pair_state, pair_gain).astype(jnp.bfloat16)
    left_edges = gated_branch(normed, left_weight, pair_mask)
    right_edges = gated_branch(normed, right_weight, pair_mask)
    mixed_pairs = jnp.einsum('ikc,jkc->ijc', left_edges.astype(jnp.float32), right_edges.astype(jnp.float32))
    mixed_norm = normalize(mixed_pairs, mix_gain).astype(jnp.bfloat16)
    gate_value = jax.nn.sigmoid(project_pairs(normed, gate_weight))
    update = project_pairs(mixed_norm, out_weight)
    pair_new = (pair_state.astype(jnp.float32) + gate_value * update).astype(jnp.bfloat16)
    bias_input = normalize(pair_new, None).astype(jnp.bfloat16)
    pair_bias = jnp.transpose(project_pairs(bias_input, bias_weight), (2, 0, 1))
    projected = jnp.dot(single_rep.reshape(-1, D), token_weight, preferred_element_type=jnp.float32)
    projected = projected.astype(jnp.bfloat16).reshape(SAMPLES, TOKENS, 3 * D)
    token_ids = jnp.arange(TOKENS, dtype=jnp.int32)
    allowed = (valid_all[None, :] > 0.5) & (chain_ids[:, None] == chain_ids[None, :]) | (token_ids[:, None] == token_ids[None, :])
    score_scale = 1.0 / math.sqrt(HEAD_DIM)

    def attend(sample_block):
        query_heads = sample_block[:, :D].astype(jnp.float32).reshape(TOKENS, HEADS, HEAD_DIM)
        key_heads = sample_block[:, D:2 * D].astype(jnp.float32).reshape(TOKENS, HEADS, HEAD_DIM)
        value_heads = sample_block[:, 2 * D:].astype(jnp.float32).reshape(TOKENS, HEADS, HEAD_DIM)
        scores = jnp.einsum('ihd,jhd->hij', query_heads, key_heads) * score_scale + pair_bias
        row_max = lax.optimization_barrier(jnp.max(jnp.where(allowed[None], scores, -1e+30), axis=-1))
        weights = jnp.where(allowed[None], jnp.exp(scores - row_max[..., None]), 0.0).astype(jnp.bfloat16)
        totals = lax.optimization_barrier(jnp.sum(weights.astype(jnp.float32), axis=-1))
        summed = jnp.einsum('hij,jhd->ihd', weights.astype(jnp.float32), value_heads)
        attended = (summed / jnp.transpose(totals)[:, :, None]).astype(jnp.bfloat16).reshape(TOKENS, D)
        return jnp.dot(attended, merge_weight, preferred_element_type=jnp.float32).astype(jnp.bfloat16)
    attention_out = lax.map(attend, projected)
    return (pair_new.reshape(TOKENS, N_ROW, N_COL, TOK_FLAT, C), attention_out)
```

```python
import functools
import math

import jax
import jax.numpy as jnp
from jax import lax
from jax.experimental import pallas as pl
from jax.experimental.pallas import tpu as pltpu
from jax.sharding import PartitionSpec as P

epsilon = 1e-05
AXES = ("row", "col")
SUB = 8
LANES = 128
VMEM_LIMIT = 56 * 1024 * 1024
EXCLUDED = -1e30


def layer_norm(values, gain):
    mean = jnp.mean(values, axis=-1, keepdims=True)
    centered = values - mean
    variance = jnp.mean(centered * centered, axis=-1, keepdims=True)
    scaled = centered * lax.rsqrt(variance + epsilon)
    return scaled if gain is None else scaled * gain


def sigmoid(values):
    return 0.5 * jnp.tanh(0.5 * values) + 0.5


def gated(normed, weight):
    width = weight.shape[1] // 2
    hidden = jnp.dot(normed, weight, preferred_element_type=jnp.float32)
    return sigmoid(hidden[:, :width]) * hidden[:, width:]


def right_kernel(first_ref, mask_ref, pair_ref, valid_ref, gain_ref, weight_ref, right_ref):
    rows = pair_ref.shape[0]
    gain = gain_ref[...]
    weight = weight_ref[...]
    valid = valid_ref[...]

    def row(i, carry):
        normed = layer_norm(pair_ref[i].astype(jnp.float32), gain).astype(jnp.bfloat16)
        own = (mask_ref[first_ref[0] + i] == 1).astype(jnp.float32)
        right_ref[i] = (gated(normed, weight) * (valid * own)).astype(jnp.bfloat16)
        return carry

    lax.fori_loop(0, rows, row, 0, unroll=2)


def left_kernel(
    block_count, meta_ref, mask_ref, same_ref, other_ref, gain_ref, weight_ref,
    left_ref, tile_ref, floats,
):
    rows, tokens, channels = same_ref.shape
    gain = gain_ref[...]
    weight = weight_ref[...]
    row_index, col_index, same_col = meta_ref[0], meta_ref[1], meta_ref[2]
    col_count = meta_ref[3]
    floats[:, tokens:] = jnp.zeros((rows, SUB, channels), jnp.float32)
    for chunk, pair_ref in enumerate((same_ref, other_ref)):
        chunk_col = same_col ^ chunk
        base = (chunk_col % 2) * rows
        first = (row_index * col_count + chunk_col) * rows

        def row(i, carry):
            values = pair_ref[i].astype(jnp.float32)
            floats[i, :tokens] = values
            normed = layer_norm(values, gain).astype(jnp.bfloat16)
            own = (mask_ref[first + i] == 1).astype(jnp.float32)
            left_ref[base + i] = (gated(normed, weight) * own).astype(jnp.bfloat16)
            return carry

        lax.fori_loop(0, rows, row, 0, unroll=2)
        for i in range(rows):
            for block in range(block_count):
                start = ((row_index ^ block) * col_count + col_index) * rows
                tile_ref[base + i, block] = floats[i, pl.ds(start, SUB), :]


def tile_kernel(block_count, carried, meta_ref, left_ref, *refs):
    right_refs = refs[:block_count]
    refs = refs[block_count:]
    tile_ref, gain_ref, mix_ref, gate_ref, out_ref, bias_ref = refs[:6]
    new_ref, head_ref, left_f, right_f, mixed_f = refs[6 + 2 * carried :]
    pair_rows, tokens, channels = left_ref.shape
    rows = pair_rows // 2
    row_index = meta_ref[0]
    left_f[...] = left_ref[...].astype(jnp.float32)
    for block in range(block_count):
        right_f[block * rows : (block + 1) * rows] = right_refs[block][...].astype(jnp.float32)
    mixed_f[:, :, rows:, :] = jnp.zeros((pair_rows, block_count, SUB - rows, channels), jnp.float32)

    def step(n, carry):
        block, half = n // 2, n % 2

        def slab(k, sums):
            at = pl.ds(pl.multiple_of(k * SUB, SUB), SUB)
            lefts = [left_f[half * rows + i, at, :] for i in range(rows)]
            rights = [right_f[block * rows + t, at, :] for t in range(rows)]
            return tuple(
                sums[i * rows + t] + lefts[i] * rights[t] for i in range(rows) for t in range(rows)
            )

        zero = jnp.zeros((SUB, channels), jnp.float32)
        sums = lax.fori_loop(0, tokens // SUB, slab, (zero,) * (rows * rows), unroll=4)
        for i in range(rows):
            for t in range(rows):
                mixed_f[half * rows + i, block, t : t + 1, :] = jnp.sum(
                    sums[i * rows + t], axis=0, keepdims=True
                )
        return carry

    lax.fori_loop(0, 2 * block_count, step, 0)
    flat = pair_rows * block_count * SUB
    mixed = mixed_f[...].reshape(flat, channels)
    mixed_norm = layer_norm(mixed, mix_ref[...]).astype(jnp.bfloat16)
    pair = tile_ref[...].reshape(flat, channels)
    normed = layer_norm(pair, gain_ref[...]).astype(jnp.bfloat16)
    gate = sigmoid(jnp.dot(normed, gate_ref[...], preferred_element_type=jnp.float32))
    update = jnp.dot(mixed_norm, out_ref[...], preferred_element_type=jnp.float32)
    pair_new = (pair + gate * update).astype(jnp.bfloat16).astype(jnp.float32)
    split = pair_new.reshape(pair_rows, block_count, SUB, channels)
    for block in range(block_count):
        new_ref[:, row_index ^ block, 0] = split[:, block, :rows, :].astype(jnp.bfloat16)
    bias_input = layer_norm(pair_new, None).astype(jnp.bfloat16)
    bias = lax.dot_general(
        bias_ref[...], bias_input, (((1,), (1,)), ((), ())), preferred_element_type=jnp.float32
    )
    head_ref[0] = bias.astype(jnp.bfloat16)


def project_kernel(block_count, meta_ref, *refs):
    single_refs = refs[:block_count]
    weight_ref, query_ref, key_ref, value_ref, rows_f, own_f = refs[block_count:]
    col_count, samples, rows, width = single_refs[0].shape
    rows_f[...] = jnp.zeros_like(rows_f)
    own_f[...] = jnp.zeros_like(own_f)
    for col in range(col_count):
        for block in range(block_count):
            at = col * block_count + block
            values = single_refs[block][col].astype(jnp.float32)
            for s in range(samples):
                rows_f[s, at, :rows, :] = values[s]
                if block == 0:
                    own_f[s, meta_ref[1] ^ col, :rows, :] = values[s]
    for s in range(samples):
        own = own_f[s].reshape(-1, width).astype(jnp.bfloat16)
        query_ref[s] = jnp.dot(
            own, weight_ref[:, :width], preferred_element_type=jnp.float32
        ).astype(jnp.bfloat16)
        full = rows_f[s].reshape(-1, width).astype(jnp.bfloat16)
        for target, at in ((key_ref, width), (value_ref, 2 * width)):
            product = jnp.dot(
                full, weight_ref[:, at : at + width], preferred_element_type=jnp.float32
            )
            target[s] = product.T.astype(jnp.bfloat16)


def attend_kernel(col_count, token_rows, head_count, query_ref, key_ref, value_ref, *refs):
    bias_refs = refs[:col_count]
    allowed_ref, merge_ref, result_ref, bias_f, joined = refs[col_count:]
    samples, query_rows, width = query_ref.shape
    key_count = key_ref.shape[2]
    head_width = width // head_count
    scale = 1.0 / math.sqrt(head_width)
    part = key_count // col_count
    group = LANES // part
    pairs = bias_refs[0].shape[0]
    lane_tiles = bias_refs[0].shape[2] // LANES
    lane = lax.broadcasted_iota(jnp.int32, (head_count, LANES), 1) // part
    for col in range(col_count):
        for t in range(token_rows, SUB):
            bias_f[col * SUB + t] = jnp.zeros((head_count, key_count), jnp.float32)
    for pair in range(pairs):
        for tile in range(lane_tiles):
            pieces = [
                ref[pair, :, tile * LANES : (tile + 1) * LANES].astype(jnp.float32)
                for ref in bias_refs
            ]
            for m in range(group):
                inside = tile * group + m
                col = 2 * pair + inside // token_rows
                row = col * SUB + inside % token_rows
                for target in range(col_count // group):
                    total = None
                    for u in range(group):
                        piece = pieces[target * group + u]
                        shift = ((u - m) * part) % LANES
                        if shift:
                            piece = pltpu.roll(piece, shift, 1)
                        total = piece if total is None else jnp.where(lane == u, piece, total)
                    bias_f[row, :, target * LANES : (target + 1) * LANES] = total
    allowed = allowed_ref[...]
    for h in range(head_count):
        at = slice(h * head_width, (h + 1) * head_width)
        bias = bias_f[:, h, :] + allowed
        for s in range(samples):
            scores = jnp.dot(
                query_ref[s, :, at], key_ref[s, at, :], preferred_element_type=jnp.float32
            )
            scores = scores * scale + bias
            weights = jnp.exp(scores - jnp.max(scores, axis=-1, keepdims=True))
            weights = weights.astype(jnp.bfloat16)
            total = jnp.sum(weights.astype(jnp.float32), axis=-1, keepdims=True)
            summed = lax.dot_general(
                weights, value_ref[s, at, :], (((1,), (1,)), ((), ())),
                preferred_element_type=jnp.float32,
            )
            joined[s, :, at] = summed / total
    merge = merge_ref[...]
    for s in range(samples):
        merged = jnp.dot(
            joined[s].astype(jnp.bfloat16), merge, preferred_element_type=jnp.float32
        )
        split = merged.reshape(col_count, SUB, width)
        result_ref[:, s] = split[:, :token_rows, :].astype(jnp.bfloat16)


def params():
    return pltpu.CompilerParams(vmem_limit_bytes=VMEM_LIMIT)


def cost(flops, moved):
    return pl.CostEstimate(flops=flops, bytes_accessed=moved, transcendentals=0)


def whole(shape):
    return pl.BlockSpec(shape, lambda *_: (0,) * len(shape))


def shards(
    pair_state,
    single_rep,
    token_mask,
    chain_ids,
    pair_gain,
    mix_gain,
    left_weight,
    right_weight,
    gate_weight,
    out_weight,
    bias_weight,
    token_weight,
    merge_weight,
):
    row_count = lax.axis_size("row")
    col_count = lax.axis_size("col")
    row_index = lax.axis_index("row")
    col_index = lax.axis_index("col")
    rows, tokens, channels = pair_state.shape
    samples, _, width = single_rep.shape
    heads = bias_weight.shape[1]
    chips = col_count // 2
    own_samples = samples // col_count
    keys = tokens // rows * SUB
    part = row_count * SUB
    core = col_index % 2
    chip = col_index // 2

    def send(values, by_row, by_col):
        steps = [
            (r * col_count + c, (r ^ by_row) * col_count + (c ^ by_col))
            for r in range(row_count)
            for c in range(col_count)
        ]
        return lax.ppermute(values, AXES, steps)

    gain = pair_gain.reshape(1, channels)
    mix = mix_gain.reshape(1, channels)
    valid = (token_mask == 1).astype(jnp.float32)

    first = ((row_index * col_count + col_index) * rows).astype(jnp.int32)[None]
    right_own = pl.pallas_call(
        right_kernel,
        grid_spec=pltpu.PrefetchScalarGridSpec(
            num_scalar_prefetch=2,
            grid=(1,),
            in_specs=[
                whole(pair_state.shape), whole((tokens, 1)), whole(gain.shape),
                whole(right_weight.shape),
            ],
            out_specs=whole(pair_state.shape),
        ),
        out_shape=jax.ShapeDtypeStruct(pair_state.shape, jnp.bfloat16),
        compiler_params=params(),
        name="right_rows",
    )(first, token_mask, pair_state, valid[:, None], gain, right_weight)
    rights = [right_own] + [send(right_own, k, 0) for k in range(1, row_count)]

    same = [pair_state] + [send(pair_state, 0, 2 * k) for k in range(1, chips)]
    other = [send(values, 0, 1) for values in same]

    by_chip = single_rep.reshape(chips, 2, own_samples, rows, width)
    arrived = []
    for k in range(chips):
        piece = lax.dynamic_index_in_dim(by_chip, chip ^ k, 0, False)
        arrived.append(send(piece, 0, 2 * k) if k else piece)
    arrived = jnp.stack(arrived)
    kept = lax.dynamic_index_in_dim(arrived, core, 1, False)
    crossed = send(lax.dynamic_index_in_dim(arrived, 1 - core, 1, False), 0, 1)
    block_single = jnp.stack([kept, crossed], axis=1).reshape(
        col_count, own_samples, rows, width
    )
    singles = [block_single] + [send(block_single, k, 0) for k in range(1, row_count)]

    def meta_of(k):
        return jnp.stack(
            [row_index, col_index, col_index ^ (2 * k), jnp.int32(col_count), chip ^ k]
        ).astype(jnp.int32)

    query_rows = col_count * SUB
    queries, key_cols, value_cols = pl.pallas_call(
        functools.partial(project_kernel, row_count),
        grid_spec=pltpu.PrefetchScalarGridSpec(
            num_scalar_prefetch=1,
            grid=(1,),
            in_specs=[whole(block_single.shape)] * row_count + [whole(token_weight.shape)],
            out_specs=[
                whole((own_samples, query_rows, width)),
                whole((own_samples, width, keys)),
                whole((own_samples, width, keys)),
            ],
            scratch_shapes=[
                pltpu.VMEM((own_samples, keys // SUB, SUB, width), jnp.float32),
                pltpu.VMEM((own_samples, col_count, SUB, width), jnp.float32),
            ],
        ),
        out_shape=[
            jax.ShapeDtypeStruct((own_samples, query_rows, width), jnp.bfloat16),
            jax.ShapeDtypeStruct((own_samples, width, keys), jnp.bfloat16),
            jax.ShapeDtypeStruct((own_samples, width, keys), jnp.bfloat16),
        ],
        compiler_params=params(),
        name="project_tokens",
    )(meta_of(0), *singles, token_weight)

    inner = jnp.arange(SUB, dtype=jnp.int32)
    col_order = jnp.arange(col_count, dtype=jnp.int32) ^ col_index
    row_order = jnp.arange(row_count, dtype=jnp.int32) ^ row_index
    key_ids = (
        (row_order[None, :, None] * col_count + col_order[:, None, None]) * rows + inner
    ).reshape(keys)
    key_real = jnp.broadcast_to(inner < rows, (col_count, row_count, SUB)).reshape(keys)
    query_ids = (
        (row_index * col_count + jnp.arange(col_count, dtype=jnp.int32)[:, None]) * rows + inner
    ).reshape(query_rows)
    token_ids = jnp.arange(tokens, dtype=jnp.int32)

    def pick(ids, table):
        return jnp.sum(jnp.where(ids[:, None] == token_ids[None, :], table[None, :], 0), axis=1)

    key_chain = pick(key_ids, chain_ids)
    key_valid = pick(key_ids, (token_mask == 1).astype(jnp.int32))
    query_chain = pick(query_ids, chain_ids)
    allowed = (key_valid[None, :] > 0) & (query_chain[:, None] == key_chain[None, :]) | (
        query_ids[:, None] == key_ids[None, :]
    )
    allowed = jnp.where(allowed & key_real[None, :], 0.0, EXCLUDED).astype(jnp.float32)

    bias_rows = bias_weight.T
    new_shape = (rows * col_count, row_count, 1, rows, channels)
    head_shape = (chips, heads, 2 * rows * part)
    pair_new = pair_heads = None
    for k in range(chips):
        meta = meta_of(k)
        left_rows, tile = pl.pallas_call(
            functools.partial(left_kernel, row_count),
            grid_spec=pltpu.PrefetchScalarGridSpec(
                num_scalar_prefetch=2,
                grid=(1,),
                in_specs=[
                    whole(pair_state.shape), whole(pair_state.shape), whole(gain.shape),
                    whole(left_weight.shape),
                ],
                out_specs=[
                    whole((2 * rows, tokens, channels)),
                    whole((2 * rows, row_count, SUB, channels)),
                ],
                scratch_shapes=[pltpu.VMEM((rows, tokens + SUB, channels), jnp.float32)],
            ),
            out_shape=[
                jax.ShapeDtypeStruct((2 * rows, tokens, channels), jnp.bfloat16),
                jax.ShapeDtypeStruct((2 * rows, row_count, SUB, channels), jnp.float32),
            ],
            compiler_params=params(),
            name=f"left_rows_{k}",
        )(meta, token_mask, same[k], other[k], gain, left_weight)
        carried = [] if pair_new is None else [pair_new, pair_heads]
        operands = [left_rows, *rights, tile, gain, mix, gate_weight, out_weight, bias_rows]
        place = 1 + len(operands)
        pair_new, pair_heads = pl.pallas_call(
            functools.partial(tile_kernel, row_count, len(carried) // 2),
            grid_spec=pltpu.PrefetchScalarGridSpec(
                num_scalar_prefetch=1,
                grid=(1,),
                in_specs=[whole(x.shape) for x in operands]
                + [pl.BlockSpec(memory_space=pl.ANY)] * len(carried),
                out_specs=[
                    pl.BlockSpec(
                        (2 * rows,) + new_shape[1:], lambda _, ref: (ref[4], 0, 0, 0, 0)
                    ),
                    pl.BlockSpec((1,) + head_shape[1:], lambda _, ref: (ref[4], 0, 0)),
                ],
                scratch_shapes=[
                    pltpu.VMEM((2 * rows, tokens, channels), jnp.float32),
                    pltpu.VMEM((rows * row_count, tokens, channels), jnp.float32),
                    pltpu.VMEM((2 * rows, row_count, SUB, channels), jnp.float32),
                ],
            ),
            out_shape=[
                jax.ShapeDtypeStruct(new_shape, jnp.bfloat16),
                jax.ShapeDtypeStruct(head_shape, jnp.bfloat16),
            ],
            input_output_aliases={place: 0, place + 1: 1} if carried else {},
            compiler_params=params(),
            name=f"pair_tile_{k}",
        )(meta, *operands, *carried)

    near = [pair_heads] + [send(pair_heads, 0, 2 * k) for k in range(1, chips)]
    biases = []
    for values in near:
        biases += [values, send(values, 0, 1)]

    merged = pl.pallas_call(
        functools.partial(attend_kernel, col_count, rows, heads),
        out_shape=jax.ShapeDtypeStruct((col_count, own_samples, rows, width), jnp.bfloat16),
        scratch_shapes=[
            pltpu.VMEM((query_rows, heads, keys), jnp.float32),
            pltpu.VMEM((own_samples, query_rows, width), jnp.float32),
        ],
        compiler_params=params(),
        name="attend",
    )(queries, key_cols, value_cols, *biases, allowed, merge_weight)
    attention_out = lax.all_to_all(merged, "col", 0, 0, tiled=True)
    return pair_new, attention_out.reshape(samples, rows, width)


def solution(mesh):
    in_specs = (
        P(("row", "col"), None, None),
        P(None, ("row", "col"), None),
    ) + (P(),) * 11
    out_specs = (P("row", None, "col", None, None), P(None, ("row", "col"), None))
    return jax.shard_map(shards, mesh=mesh, in_specs=in_specs, out_specs=out_specs, check_vma=False)
```

```python
import functools
import math

import jax
import jax.numpy as jnp
from jax import lax
from jax.experimental import pallas as pl
from jax.experimental.pallas import tpu as pltpu
from jax.sharding import PartitionSpec as P

epsilon = 1e-05
AXES = ("row", "col")
SUB = 8
LANES = 128
FLAT_ROWS = 1152
EXCLUDED = -1e30
SCALARS = pl.BlockSpec(memory_space=pltpu.SMEM)
BLOCK = pl.BlockSpec(memory_space=pltpu.VMEM)


def layer_norm(values, gain):
    mean = jnp.mean(values, axis=-1, keepdims=True)
    centered = values - mean
    variance = jnp.mean(centered * centered, axis=-1, keepdims=True)
    scaled = centered * lax.rsqrt(variance + epsilon)
    return scaled if gain is None else scaled * gain


def sigmoid(values):
    return 0.5 * jnp.tanh(0.5 * values) + 0.5


def gated(normed, weight):
    width = weight.shape[1] // 2
    hidden = jnp.dot(normed, weight, preferred_element_type=jnp.float32)
    return sigmoid(hidden[:, :width]) * hidden[:, width:]


def edge_rows(values, gain, weight):
    count, tokens, channels = values.shape
    flat = layer_norm(values.reshape(count * tokens, channels), gain).astype(jnp.bfloat16)
    return gated(flat, weight).reshape(count, tokens, channels)


def in_groups(rows, tokens, step):
    group = max(1, min(rows, FLAT_ROWS // tokens))
    while rows % group:
        group -= 1
    if group == rows:
        step(0, rows)
    else:
        lax.fori_loop(0, rows // group, lambda g, carry: (step(g * group, group), carry)[1], 0)


def right_kernel(place_ref, mask_ref, valid_ref, gain_ref, weight_ref, *refs):
    pair_refs, right_ref = refs[:-1], refs[-1]
    rows, tokens, channels = pair_refs[0].shape
    gain = gain_ref[...]
    weight = weight_ref[...]
    row_index, col_index, col_count = place_ref[0], place_ref[1], place_ref[2]
    valid = jnp.broadcast_to((valid_ref[...] == 1).astype(jnp.float32), (channels, tokens)).T
    for block, pair_ref in enumerate(pair_refs):
        first = ((row_index ^ block) * col_count + col_index) * rows

        def step(start, count):
            edges = edge_rows(pair_ref[pl.ds(start, count)].astype(jnp.float32), gain, weight)
            for i in range(count):
                own = (mask_ref[first + start + i] == 1).astype(jnp.float32)
                right_ref[block * rows + start + i] = (
                    (edges[i] * (valid * own)).astype(jnp.bfloat16).astype(jnp.float32)
                )

        in_groups(rows, tokens, step)


def pair_kernel(block_count, step_at, earlier, place_ref, mask_ref, *refs):
    same_ref, other_ref, right_ref = refs[:3]
    gain_ref, mix_ref, left_ref, gate_ref, out_ref, bias_ref = refs[3:9]
    given = refs[9 : 9 + 2 * len(earlier)]
    new_ref, head_ref, left_f, floats, tile_f, mixed_f = refs[9 + 2 * len(earlier) :]
    rows, tokens, channels = same_ref.shape
    pair_rows = 2 * rows
    gain = gain_ref[...]
    weight = left_ref[...]
    row_index, col_index, col_count = place_ref[0], place_ref[1], place_ref[2]
    floats[:, tokens:] = jnp.zeros((rows, SUB, channels), jnp.float32)
    for chunk, pair_ref in enumerate((same_ref, other_ref)):
        chunk_col = col_index ^ (2 * step_at + chunk)
        base = (chunk_col % 2) * rows
        first = (row_index * col_count + chunk_col) * rows

        def step(start, count):
            values = pair_ref[pl.ds(start, count)].astype(jnp.float32)
            floats[pl.ds(start, count), :tokens] = values
            edges = edge_rows(values, gain, weight)
            for i in range(count):
                own = (mask_ref[first + start + i] == 1).astype(jnp.float32)
                left_f[base + start + i] = (
                    (edges[i] * own).astype(jnp.bfloat16).astype(jnp.float32)
                )

        in_groups(rows, tokens, step)
        for i in range(rows):
            for block in range(block_count):
                start = ((row_index ^ block) * col_count + col_index) * rows
                tile_f[base + i, block] = floats[i, pl.ds(start, SUB), :]
    mixed_f[:, :, rows:, :] = jnp.zeros((pair_rows, block_count, SUB - rows, channels), jnp.float32)

    def product(n, carry):
        block, half = n // 2, n % 2

        def slab(k, sums):
            at = pl.ds(pl.multiple_of(k * SUB, SUB), SUB)
            lefts = [left_f[half * rows + i, at, :] for i in range(rows)]
            rights = [right_ref[block * rows + t, at, :] for t in range(rows)]
            return tuple(
                sums[i * rows + t] + lefts[i] * rights[t] for i in range(rows) for t in range(rows)
            )

        zero = jnp.zeros((SUB, channels), jnp.float32)
        sums = lax.fori_loop(0, tokens // SUB, slab, (zero,) * (rows * rows), unroll=24)
        for i in range(rows):
            for t in range(rows):
                mixed_f[half * rows + i, block, t : t + 1, :] = jnp.sum(
                    sums[i * rows + t], axis=0, keepdims=True
                )
        return carry

    lax.fori_loop(0, 2 * block_count, product, 0)
    flat = pair_rows * block_count * SUB
    mixed_norm = layer_norm(mixed_f[...].reshape(flat, channels), mix_ref[...]).astype(jnp.bfloat16)
    pair = tile_f[...].reshape(flat, channels)
    normed = layer_norm(pair, gain).astype(jnp.bfloat16)
    gate = sigmoid(jnp.dot(normed, gate_ref[...], preferred_element_type=jnp.float32))
    update = jnp.dot(mixed_norm, out_ref[...], preferred_element_type=jnp.float32)
    pair_new = (pair + gate * update).astype(jnp.bfloat16).astype(jnp.float32)
    split = pair_new.reshape(pair_rows, block_count, SUB, channels)
    bias_input = layer_norm(pair_new, None).astype(jnp.bfloat16)
    bias = lax.dot_general(
        bias_ref[...], bias_input, (((0,), (1,)), ((), ())), preferred_element_type=jnp.float32
    )
    joins = new_ref.shape[0] > pair_rows
    chip = col_index // 2
    place = chip ^ step_at if joins else 0
    for block in range(block_count):
        new_ref[pl.ds(place * pair_rows, pair_rows), row_index ^ block, 0] = split[
            :, block, :rows, :
        ].astype(jnp.bfloat16)
    head_ref[place] = bias.astype(jnp.bfloat16)
    for n, k in enumerate(earlier):
        new_ref[pl.ds((chip ^ k) * pair_rows, pair_rows)] = given[2 * n][...]
        head_ref[chip ^ k] = given[2 * n + 1][0]


def project_kernel(block_count, place_ref, chain_ref, valid_ref, weight_ref, *refs):
    single_refs = refs[:block_count]
    query_ref, key_ref, value_ref, allowed_ref, rows_f, own_f = refs[block_count:]
    col_count, rows, samples, width = single_refs[0].shape
    query_rows, key_count = allowed_ref.shape
    tokens = chain_ref.shape[1]
    row_index, col_index = place_ref[0], place_ref[1]
    rows_f[...] = jnp.zeros_like(rows_f)
    own_f[...] = jnp.zeros_like(own_f)
    for col in range(col_count):
        for block in range(block_count):
            at = col * block_count + block
            for t in range(rows):
                values = single_refs[block][col_index ^ col, t].astype(jnp.float32)
                for s in range(samples):
                    rows_f[s, at, t : t + 1, :] = values[s : s + 1]
        for t in range(rows):
            values = single_refs[0][col, t].astype(jnp.float32)
            for s in range(samples):
                own_f[s, col, t : t + 1, :] = values[s : s + 1]
    for s in range(samples):
        own = own_f[s].reshape(-1, width).astype(jnp.bfloat16)
        query_ref[s] = jnp.dot(
            own, weight_ref[:, :width], preferred_element_type=jnp.float32
        ).astype(jnp.bfloat16)
        full = rows_f[s].reshape(-1, width).astype(jnp.bfloat16)
        for target, at in ((key_ref, width), (value_ref, 2 * width)):
            product = jnp.dot(
                full, weight_ref[:, at : at + width], preferred_element_type=jnp.float32
            )
            target[s] = product.T.astype(jnp.bfloat16)

    def key_tokens(shape, axis):
        place = lax.broadcasted_iota(jnp.int32, shape, axis)
        t = place % SUB
        block = (place // SUB) % block_count
        col = place // (SUB * block_count)
        token = ((row_index ^ block) * col_count + (col_index ^ col)) * rows + t
        return jnp.where(t < rows, token, -1)

    def query_tokens(shape):
        place = lax.broadcasted_iota(jnp.int32, shape, 0)
        t = place % SUB
        token = (row_index * col_count + place // SUB) * rows + t
        return jnp.where(t < rows, token, -2)

    chains = chain_ref[...].astype(jnp.float32)
    valid = (valid_ref[...] == 1).astype(jnp.float32)
    token = lax.broadcasted_iota(jnp.int32, (query_rows, tokens), 1)
    hit = query_tokens((query_rows, tokens)) == token
    query_chain = jnp.sum(jnp.where(hit, chains, 0.0), axis=1, keepdims=True)
    token = lax.broadcasted_iota(jnp.int32, (key_count, tokens), 1)
    hit = jnp.where(key_tokens((key_count, tokens), 0) == token, 1.0, 0.0).astype(jnp.bfloat16)

    def of_keys(table):
        table = jnp.broadcast_to(table, (SUB, tokens)).astype(jnp.bfloat16)
        return lax.dot_general(
            table, hit, (((1,), (1,)), ((), ())), preferred_element_type=jnp.float32
        )[:1]

    keys = key_tokens((query_rows, key_count), 1)
    near = (of_keys(valid) > 0.5) & (of_keys(chains) == query_chain) & (keys >= 0)
    allowed = near | (keys == query_tokens((query_rows, key_count)))
    allowed_ref[...] = jnp.where(allowed, 0.0, EXCLUDED)


def attend_kernel(col_count, token_rows, head_count, query_ref, key_ref, value_ref, *refs):
    bias_refs = refs[:col_count]
    allowed_ref, merge_ref, result_ref, bias_f, joined = refs[col_count:]
    samples, query_rows, width = query_ref.shape
    key_count = key_ref.shape[2]
    head_width = width // head_count
    scale = 1.0 / math.sqrt(head_width)
    part = key_count // col_count
    group = LANES // part
    pairs = bias_refs[0].shape[0]
    lane_tiles = bias_refs[0].shape[2] // LANES
    lane = lax.broadcasted_iota(jnp.int32, (head_count, LANES), 1) // part
    for col in range(col_count):
        for t in range(token_rows, SUB):
            bias_f[col * SUB + t] = jnp.zeros((head_count, key_count), jnp.float32)
    for pair in range(pairs):
        for tile in range(lane_tiles):
            pieces = [
                ref[pair, :, tile * LANES : (tile + 1) * LANES].astype(jnp.float32)
                for ref in bias_refs
            ]
            for m in range(group):
                inside = tile * group + m
                col = 2 * pair + inside // token_rows
                row = col * SUB + inside % token_rows
                for target in range(col_count // group):
                    total = None
                    for u in range(group):
                        piece = pieces[target * group + u]
                        shift = ((u - m) * part) % LANES
                        if shift:
                            piece = pltpu.roll(piece, shift, 1)
                        total = piece if total is None else jnp.where(lane == u, piece, total)
                    bias_f[row, :, target * LANES : (target + 1) * LANES] = total
    allowed = allowed_ref[...]
    parts = [[] for _ in range(samples)]
    for h in range(head_count):
        at = slice(h * head_width, (h + 1) * head_width)
        bias = bias_f[:, h, :] + allowed
        for s in range(samples):
            scores = jnp.dot(
                query_ref[s, :, at], key_ref[s, at, :], preferred_element_type=jnp.float32
            )
            scores = scores * scale + bias
            weights = jnp.exp(scores - jnp.max(scores, axis=-1, keepdims=True))
            weights = weights.astype(jnp.bfloat16)
            total = jnp.sum(weights.astype(jnp.float32), axis=-1, keepdims=True)
            summed = lax.dot_general(
                weights, value_ref[s, at, :], (((1,), (1,)), ((), ())),
                preferred_element_type=jnp.float32,
            )
            parts[s].append(summed / total)
    lane_parts = range(width // LANES)
    for s in range(samples):
        attended = jnp.concatenate(parts[s], axis=1)
        for n in lane_parts:
            joined[n, pl.ds(s, query_rows, stride=samples), :] = attended[
                :, n * LANES : (n + 1) * LANES
            ]
    attended = jnp.concatenate([joined[n] for n in lane_parts], axis=1).astype(jnp.bfloat16)
    merged = jnp.dot(attended, merge_ref[...], preferred_element_type=jnp.float32)
    split = merged.reshape(col_count, SUB * samples, width)
    result_ref[...] = split[:, : token_rows * samples, :].astype(jnp.bfloat16)


def call(kernel, name, operands, scalars, outs, scratch, time_us):
    def size(shape, kind):
        return math.prod(shape) * jnp.dtype(kind).itemsize

    held = sum(size(x.shape, x.dtype) for x in operands) + sum(size(*x) for x in outs)
    work = sum(size(*x) for x in scratch)
    limit = min(60 << 20, int(1.25 * (held + work)) + (6 << 20))
    return pl.pallas_call(
        kernel,
        in_specs=[SCALARS] * scalars + [BLOCK] * (len(operands) - scalars),
        out_specs=[BLOCK] * len(outs),
        out_shape=[jax.ShapeDtypeStruct(*x) for x in outs],
        scratch_shapes=[pltpu.VMEM(*x) for x in scratch],
        cost_estimate=pl.CostEstimate(
            flops=0, bytes_accessed=int(time_us * 3.6e6), transcendentals=0
        ),
        compiler_params=pltpu.CompilerParams(vmem_limit_bytes=limit),
        name=name,
    )(*operands)


def shards(
    pair_state,
    single_rep,
    token_mask,
    chain_ids,
    pair_gain,
    mix_gain,
    left_weight,
    right_weight,
    gate_weight,
    out_weight,
    bias_weight,
    token_weight,
    merge_weight,
):
    row_count = lax.axis_size("row")
    col_count = lax.axis_size("col")
    row_index = lax.axis_index("row")
    col_index = lax.axis_index("col")
    rows, tokens, channels = pair_state.shape
    samples, _, width = single_rep.shape
    heads = bias_weight.shape[1]
    chips = col_count // 2
    own_samples = samples // col_count
    keys = tokens // rows * SUB
    query_rows = col_count * SUB
    part = row_count * SUB
    bf16, f32 = jnp.bfloat16, jnp.float32

    def send(values, by_row, by_col):
        steps = [
            (r * col_count + c, (r ^ by_row) * col_count + (c ^ by_col))
            for r in range(row_count)
            for c in range(col_count)
        ]
        return lax.ppermute(values, AXES, steps)

    place = jnp.stack([row_index, col_index, jnp.int32(col_count)]).astype(jnp.int32)
    gain = pair_gain.reshape(1, channels)
    mix = mix_gain.reshape(1, channels)
    valid_row = token_mask.reshape(1, tokens)
    chain_row = chain_ids.reshape(1, tokens)

    same = [pair_state] + [send(pair_state, 0, 2 * k) for k in range(1, chips)]
    other = [send(values, 0, 1) for values in same]
    columns = [pair_state] + [send(pair_state, k, 0) for k in range(1, row_count)]

    by_token = jnp.transpose(single_rep, (1, 0, 2)).reshape(rows, col_count, own_samples, width)
    own_single = lax.all_to_all(jnp.transpose(by_token, (1, 0, 2, 3)), "col", 0, 0, tiled=True)
    singles = [own_single] + [send(own_single, k, 0) for k in range(1, row_count)]

    (rights,) = call(
        right_kernel, "right_rows",
        [place, token_mask, valid_row, gain, right_weight, *columns], 2,
        [((row_count * rows, tokens, channels), f32)], [], 3.0,
    )
    done = []
    for k in range(chips):
        last = k == chips - 1
        count = chips if last else 1
        earlier = tuple(range(k)) if last else ()
        pair_new, pair_heads = call(
            functools.partial(pair_kernel, row_count, k, earlier), f"pair_rows_{k}",
            [
                place, token_mask, same[k], other[k], rights, gain, mix, left_weight,
                gate_weight, out_weight, bias_weight, *(x for n in earlier for x in done[n]),
            ], 2,
            [
                ((count * 2 * rows, row_count, 1, rows, channels), bf16),
                ((count, heads, 2 * rows * part), bf16),
            ],
            [
                ((2 * rows, tokens, channels), f32),
                ((rows, tokens + SUB, channels), f32),
                ((2 * rows, row_count, SUB, channels), f32),
                ((2 * rows, row_count, SUB, channels), f32),
            ], 4.0,
        )
        done.append((pair_new, pair_heads))

    queries, key_cols, value_cols, allowed = call(
        functools.partial(project_kernel, row_count), "project_tokens",
        [place, chain_row, valid_row, token_weight, *singles], 1,
        [
            ((own_samples, query_rows, width), bf16),
            ((own_samples, width, keys), bf16),
            ((own_samples, width, keys), bf16),
            ((query_rows, keys), f32),
        ],
        [
            ((own_samples, keys // SUB, SUB, width), f32),
            ((own_samples, col_count, SUB, width), f32),
        ], 5.0,
    )

    near = [pair_heads] + [send(pair_heads, 0, 2 * k) for k in range(1, chips)]
    biases = []
    for values in near:
        biases += [values, send(values, 0, 1)]

    (merged,) = call(
        functools.partial(attend_kernel, col_count, rows, heads), "attend",
        [queries, key_cols, value_cols, *biases, allowed, merge_weight], 0,
        [((col_count, rows * own_samples, width), bf16)],
        [((query_rows, heads, keys), f32), ((width // LANES, own_samples * query_rows, LANES), f32)], 6.0,
    )
    arrived = lax.all_to_all(merged, "col", 0, 0, tiled=True)
    arrived = arrived.reshape(col_count, rows, own_samples, width)
    attention_out = jnp.transpose(arrived, (0, 2, 1, 3)).reshape(samples, rows, width)
    return pair_new, attention_out


def solution(mesh):
    in_specs = (
        P(("row", "col"), None, None),
        P(None, ("row", "col"), None),
    ) + (P(),) * 11
    out_specs = (P("row", None, "col", None, None), P(None, ("row", "col"), None))
    return jax.shard_map(shards, mesh=mesh, in_specs=in_specs, out_specs=out_specs, check_vma=False)
```

```python
import functools
import math

import jax
import jax.numpy as jnp
from jax import lax
from jax.experimental import pallas as pl
from jax.experimental.pallas import tpu as pltpu
from jax.sharding import PartitionSpec as P

epsilon = 1e-05
AXES = ("row", "col")
SUB = 8
LANES = 128
FLAT_ROWS = 1152
EXCLUDED = -1e30
SCALARS = pl.BlockSpec(memory_space=pltpu.SMEM)
BLOCK = pl.BlockSpec(memory_space=pltpu.VMEM)


def layer_norm(values, gain):
    mean = jnp.mean(values, axis=-1, keepdims=True)
    centered = values - mean
    variance = jnp.mean(centered * centered, axis=-1, keepdims=True)
    scaled = centered * lax.rsqrt(variance + epsilon)
    return scaled if gain is None else scaled * gain


def sigmoid(values):
    return 0.5 * jnp.tanh(0.5 * values) + 0.5


def gated(normed, weight):
    width = weight.shape[1] // 2
    hidden = jnp.dot(normed, weight, preferred_element_type=jnp.float32)
    return sigmoid(hidden[:, :width]) * hidden[:, width:]


def edge_rows(values, gain, weight):
    count, tokens, channels = values.shape
    flat = layer_norm(values.reshape(count * tokens, channels), gain).astype(jnp.bfloat16)
    return gated(flat, weight).reshape(count, tokens, channels)


def in_groups(rows, tokens, step):
    group = max(1, min(rows, FLAT_ROWS // tokens))
    while rows % group:
        group -= 1
    if group == rows:
        step(0, rows)
    else:
        lax.fori_loop(0, rows // group, lambda g, carry: (step(g * group, group), carry)[1], 0)


def right_kernel(place_ref, mask_ref, table_ref, gains_ref, weight_ref, *refs):
    pair_refs, right_ref = refs[:-1], refs[-1]
    rows, tokens, channels = pair_refs[0].shape
    gain = gains_ref[0:1]
    weight = weight_ref[:, 2 * channels : 4 * channels]
    row_index, col_index, col_count = place_ref[0], place_ref[1], place_ref[2]
    valid = jnp.broadcast_to((table_ref[0:1] == 1).astype(jnp.float32), (channels, tokens)).T
    for block, pair_ref in enumerate(pair_refs):
        first = ((row_index ^ block) * col_count + col_index) * rows

        def step(start, count):
            edges = edge_rows(pair_ref[pl.ds(start, count)].astype(jnp.float32), gain, weight)
            for i in range(count):
                own = (mask_ref[first + start + i] == 1).astype(jnp.float32)
                right_ref[block * rows + start + i] = (
                    (edges[i] * (valid * own)).astype(jnp.bfloat16).astype(jnp.float32)
                )

        in_groups(rows, tokens, step)


def pair_kernel(block_count, steps, head_count, place_ref, mask_ref, *refs):
    pair_refs = refs[: 2 * steps]
    right_ref, gains_ref, weight_ref, new_ref, head_ref, left_f, floats, tile_f, mixed_f = refs[
        2 * steps :
    ]
    rows, tokens, channels = pair_refs[0].shape
    pair_rows = 2 * rows
    gain, mix = gains_ref[0:1], gains_ref[1:2]
    weight = weight_ref[:, : 2 * channels]
    gate_weight = weight_ref[:, 4 * channels : 5 * channels]
    out_weight = weight_ref[:, 5 * channels : 6 * channels]
    bias_weight = weight_ref[:, 6 * channels : 6 * channels + head_count]
    row_index, col_index, col_count = place_ref[0], place_ref[1], place_ref[2]
    floats[:, tokens:] = jnp.zeros((rows, SUB, channels), jnp.float32)
    mixed_f[:, :, rows:, :] = jnp.zeros((pair_rows, block_count, SUB - rows, channels), jnp.float32)
    chip = col_index // 2
    for step_at in range(steps):
        for chunk, pair_ref in enumerate(pair_refs[2 * step_at : 2 * step_at + 2]):
            chunk_col = col_index ^ (2 * step_at + chunk)
            base = (chunk_col % 2) * rows
            first = (row_index * col_count + chunk_col) * rows

            def step(start, count):
                values = pair_ref[pl.ds(start, count)].astype(jnp.float32)
                floats[pl.ds(start, count), :tokens] = values
                edges = edge_rows(values, gain, weight)
                for i in range(count):
                    own = (mask_ref[first + start + i] == 1).astype(jnp.float32)
                    left_f[base + start + i] = (
                        (edges[i] * own).astype(jnp.bfloat16).astype(jnp.float32)
                    )

            in_groups(rows, tokens, step)
            for i in range(rows):
                for block in range(block_count):
                    start = ((row_index ^ block) * col_count + col_index) * rows
                    tile_f[base + i, block] = floats[i, pl.ds(start, SUB), :]

        def product(n, carry):
            block, half = n // 2, n % 2

            def slab(k, sums):
                at = pl.ds(pl.multiple_of(k * SUB, SUB), SUB)
                lefts = [left_f[half * rows + i, at, :] for i in range(rows)]
                rights = [right_ref[block * rows + t, at, :] for t in range(rows)]
                return tuple(
                    sums[i * rows + t] + lefts[i] * rights[t] for i in range(rows) for t in range(rows)
                )

            zero = jnp.zeros((SUB, channels), jnp.float32)
            sums = lax.fori_loop(0, tokens // SUB, slab, (zero,) * (rows * rows), unroll=24)
            for i in range(rows):
                for t in range(rows):
                    mixed_f[half * rows + i, block, t : t + 1, :] = jnp.sum(
                        sums[i * rows + t], axis=0, keepdims=True
                    )
            return carry

        lax.fori_loop(0, 2 * block_count, product, 0)
        flat = pair_rows * block_count * SUB
        mixed_norm = layer_norm(mixed_f[...].reshape(flat, channels), mix).astype(jnp.bfloat16)
        pair = tile_f[...].reshape(flat, channels)
        normed = layer_norm(pair, gain).astype(jnp.bfloat16)
        gate = sigmoid(jnp.dot(normed, gate_weight, preferred_element_type=jnp.float32))
        update = jnp.dot(mixed_norm, out_weight, preferred_element_type=jnp.float32)
        pair_new = (pair + gate * update).astype(jnp.bfloat16).astype(jnp.float32)
        split = pair_new.reshape(pair_rows, block_count, SUB, channels)
        bias_input = layer_norm(pair_new, None).astype(jnp.bfloat16)
        bias = lax.dot_general(
            bias_weight, bias_input, (((0,), (1,)), ((), ())), preferred_element_type=jnp.float32
        )
        place = chip ^ step_at
        for block in range(block_count):
            new_ref[pl.ds(place * pair_rows, pair_rows), row_index ^ block, 0] = split[
                :, block, :rows, :
            ].astype(jnp.bfloat16)
        head_ref[place] = bias.astype(jnp.bfloat16)


def project_kernel(block_count, place_ref, table_ref, weight_ref, *refs):
    single_refs = refs[:block_count]
    query_ref, key_ref, value_ref, allowed_ref, rows_f, own_f = refs[block_count:]
    col_count, rows, samples, width = single_refs[0].shape
    query_rows, key_count = allowed_ref.shape
    tokens = table_ref.shape[1]
    row_index, col_index = place_ref[0], place_ref[1]
    rows_f[...] = jnp.zeros_like(rows_f)
    own_f[...] = jnp.zeros_like(own_f)
    for col in range(col_count):
        for block in range(block_count):
            at = col * block_count + block
            for t in range(rows):
                values = single_refs[block][col_index ^ col, t].astype(jnp.float32)
                for s in range(samples):
                    rows_f[s, at, t : t + 1, :] = values[s : s + 1]
        for t in range(rows):
            values = single_refs[0][col, t].astype(jnp.float32)
            for s in range(samples):
                own_f[s, col, t : t + 1, :] = values[s : s + 1]
    for s in range(samples):
        own = own_f[s].reshape(-1, width).astype(jnp.bfloat16)
        query_ref[s] = jnp.dot(
            own, weight_ref[:, :width], preferred_element_type=jnp.float32
        ).astype(jnp.bfloat16)
        full = rows_f[s].reshape(-1, width).astype(jnp.bfloat16)
        for target, at in ((key_ref, width), (value_ref, 2 * width)):
            product = jnp.dot(
                full, weight_ref[:, at : at + width], preferred_element_type=jnp.float32
            )
            target[s] = product.T.astype(jnp.bfloat16)

    def key_tokens(shape, axis):
        place = lax.broadcasted_iota(jnp.int32, shape, axis)
        t = place % SUB
        block = (place // SUB) % block_count
        col = place // (SUB * block_count)
        token = ((row_index ^ block) * col_count + (col_index ^ col)) * rows + t
        return jnp.where(t < rows, token, -1)

    def query_tokens(shape):
        place = lax.broadcasted_iota(jnp.int32, shape, 0)
        t = place % SUB
        token = (row_index * col_count + place // SUB) * rows + t
        return jnp.where(t < rows, token, -2)

    chains = table_ref[1:2].astype(jnp.float32)
    valid = (table_ref[0:1] == 1).astype(jnp.float32)
    token = lax.broadcasted_iota(jnp.int32, (query_rows, tokens), 1)
    hit = query_tokens((query_rows, tokens)) == token
    query_chain = jnp.sum(jnp.where(hit, chains, 0.0), axis=1, keepdims=True)
    token = lax.broadcasted_iota(jnp.int32, (key_count, tokens), 1)
    hit = jnp.where(key_tokens((key_count, tokens), 0) == token, 1.0, 0.0).astype(jnp.bfloat16)

    def of_keys(table):
        table = jnp.broadcast_to(table, (SUB, tokens)).astype(jnp.bfloat16)
        return lax.dot_general(
            table, hit, (((1,), (1,)), ((), ())), preferred_element_type=jnp.float32
        )[:1]

    keys = key_tokens((query_rows, key_count), 1)
    near = (of_keys(valid) > 0.5) & (of_keys(chains) == query_chain) & (keys >= 0)
    allowed = near | (keys == query_tokens((query_rows, key_count)))
    allowed_ref[...] = jnp.where(allowed, 0.0, EXCLUDED)


def attend_kernel(col_count, token_rows, head_count, query_ref, key_ref, value_ref, *refs):
    bias_refs = refs[:col_count]
    allowed_ref, merge_ref, result_ref, bias_f, joined = refs[col_count:]
    samples, query_rows, width = query_ref.shape
    key_count = key_ref.shape[2]
    head_width = width // head_count
    scale = 1.0 / math.sqrt(head_width)
    part = key_count // col_count
    group = LANES // part
    pairs = bias_refs[0].shape[0]
    lane_tiles = bias_refs[0].shape[2] // LANES
    lane = lax.broadcasted_iota(jnp.int32, (head_count, LANES), 1) // part
    for col in range(col_count):
        for t in range(token_rows, SUB):
            bias_f[col * SUB + t] = jnp.zeros((head_count, key_count), jnp.float32)
    for pair in range(pairs):
        for tile in range(lane_tiles):
            pieces = [
                ref[pair, :, tile * LANES : (tile + 1) * LANES].astype(jnp.float32)
                for ref in bias_refs
            ]
            for m in range(group):
                inside = tile * group + m
                col = 2 * pair + inside // token_rows
                row = col * SUB + inside % token_rows
                for target in range(col_count // group):
                    total = None
                    for u in range(group):
                        piece = pieces[target * group + u]
                        shift = ((u - m) * part) % LANES
                        if shift:
                            piece = pltpu.roll(piece, shift, 1)
                        total = piece if total is None else jnp.where(lane == u, piece, total)
                    bias_f[row, :, target * LANES : (target + 1) * LANES] = total
    allowed = allowed_ref[...]
    parts = [[] for _ in range(samples)]
    for h in range(head_count):
        at = slice(h * head_width, (h + 1) * head_width)
        bias = bias_f[:, h, :] + allowed
        for s in range(samples):
            scores = jnp.dot(
                query_ref[s, :, at], key_ref[s, at, :], preferred_element_type=jnp.float32
            )
            scores = scores * scale + bias
            weights = jnp.exp(scores - jnp.max(scores, axis=-1, keepdims=True))
            weights = weights.astype(jnp.bfloat16)
            total = jnp.sum(weights.astype(jnp.float32), axis=-1, keepdims=True)
            summed = lax.dot_general(
                weights, value_ref[s, at, :], (((1,), (1,)), ((), ())),
                preferred_element_type=jnp.float32,
            )
            parts[s].append(summed / total)
    lane_parts = range(width // LANES)
    for s in range(samples):
        attended = jnp.concatenate(parts[s], axis=1)
        for n in lane_parts:
            joined[n, pl.ds(s, query_rows, stride=samples), :] = attended[
                :, n * LANES : (n + 1) * LANES
            ]
    attended = jnp.concatenate([joined[n] for n in lane_parts], axis=1).astype(jnp.bfloat16)
    merged = jnp.dot(attended, merge_ref[...], preferred_element_type=jnp.float32)
    split = merged.reshape(col_count, SUB * samples, width)
    result_ref[...] = split[:, : token_rows * samples, :].astype(jnp.bfloat16)


def call(kernel, name, operands, scalars, outs, scratch, time_us):
    def size(shape, kind):
        return math.prod(shape) * jnp.dtype(kind).itemsize

    held = sum(size(x.shape, x.dtype) for x in operands) + sum(size(*x) for x in outs)
    work = sum(size(*x) for x in scratch)
    limit = min(60 << 20, int(1.25 * (held + work)) + (6 << 20))
    return pl.pallas_call(
        kernel,
        in_specs=[SCALARS] * scalars + [BLOCK] * (len(operands) - scalars),
        out_specs=[BLOCK] * len(outs),
        out_shape=[jax.ShapeDtypeStruct(*x) for x in outs],
        scratch_shapes=[pltpu.VMEM(*x) for x in scratch],
        cost_estimate=pl.CostEstimate(
            flops=0, bytes_accessed=int(time_us * 3.6e6), transcendentals=0
        ),
        compiler_params=pltpu.CompilerParams(vmem_limit_bytes=limit),
        name=name,
    )(*operands)


def shards(
    pair_state,
    single_rep,
    token_mask,
    chain_ids,
    pair_gain,
    mix_gain,
    left_weight,
    right_weight,
    gate_weight,
    out_weight,
    bias_weight,
    token_weight,
    merge_weight,
):
    row_count = lax.axis_size("row")
    col_count = lax.axis_size("col")
    row_index = lax.axis_index("row")
    col_index = lax.axis_index("col")
    rows, tokens, channels = pair_state.shape
    samples, _, width = single_rep.shape
    heads = bias_weight.shape[1]
    chips = col_count // 2
    own_samples = samples // col_count
    keys = tokens // rows * SUB
    query_rows = col_count * SUB
    part = row_count * SUB
    bf16, f32 = jnp.bfloat16, jnp.float32

    def send(values, by_row, by_col):
        steps = [
            (r * col_count + c, (r ^ by_row) * col_count + (c ^ by_col))
            for r in range(row_count)
            for c in range(col_count)
        ]
        return lax.ppermute(values, AXES, steps)

    place = jnp.stack([row_index, col_index, jnp.int32(col_count)]).astype(jnp.int32)
    gains = jnp.stack([pair_gain, mix_gain])
    table = jnp.stack([token_mask, chain_ids])
    bias_columns = jnp.pad(bias_weight, ((0, 0), (0, LANES - heads)))
    weights = jnp.concatenate(
        [left_weight, right_weight, gate_weight, out_weight, bias_columns], axis=1
    )

    same = [pair_state] + [send(pair_state, 0, 2 * k) for k in range(1, chips)]
    other = [send(values, 0, 1) for values in same]
    columns = [pair_state] + [send(pair_state, k, 0) for k in range(1, row_count)]

    by_token = jnp.transpose(single_rep, (1, 0, 2)).reshape(rows, col_count, own_samples, width)
    own_single = lax.all_to_all(jnp.transpose(by_token, (1, 0, 2, 3)), "col", 0, 0, tiled=True)
    singles = [own_single] + [send(own_single, k, 0) for k in range(1, row_count)]

    (rights,) = call(
        right_kernel, "right_rows",
        [place, token_mask, table, gains, weights, *columns], 2,
        [((row_count * rows, tokens, channels), f32)], [], 3.0,
    )
    pair_new, pair_heads = call(
        functools.partial(pair_kernel, row_count, chips, heads), "pair_rows",
        [
            place, token_mask, *(x for k in range(chips) for x in (same[k], other[k])), rights,
            gains, weights,
        ], 2,
        [
            ((rows * col_count, row_count, 1, rows, channels), bf16),
            ((chips, heads, 2 * rows * part), bf16),
        ],
        [
            ((2 * rows, tokens, channels), f32),
            ((rows, tokens + SUB, channels), f32),
            ((2 * rows, row_count, SUB, channels), f32),
            ((2 * rows, row_count, SUB, channels), f32),
        ], 4.0,
    )

    queries, key_cols, value_cols, allowed = call(
        functools.partial(project_kernel, row_count), "project_tokens",
        [place, table, token_weight, *singles], 1,
        [
            ((own_samples, query_rows, width), bf16),
            ((own_samples, width, keys), bf16),
            ((own_samples, width, keys), bf16),
            ((query_rows, keys), f32),
        ],
        [
            ((own_samples, keys // SUB, SUB, width), f32),
            ((own_samples, col_count, SUB, width), f32),
        ], 5.0,
    )

    near = [pair_heads] + [send(pair_heads, 0, 2 * k) for k in range(1, chips)]
    biases = []
    for values in near:
        biases += [values, send(values, 0, 1)]

    (merged,) = call(
        functools.partial(attend_kernel, col_count, rows, heads), "attend",
        [queries, key_cols, value_cols, *biases, allowed, merge_weight], 0,
        [((col_count, rows * own_samples, width), bf16)],
        [((query_rows, heads, keys), f32), ((width // LANES, own_samples * query_rows, LANES), f32)], 6.0,
    )
    arrived = lax.all_to_all(merged, "col", 0, 0, tiled=True)
    arrived = arrived.reshape(col_count, rows, own_samples, width)
    attention_out = jnp.transpose(arrived, (0, 2, 1, 3)).reshape(samples, rows, width)
    return pair_new, attention_out


def solution(mesh):
    in_specs = (
        P(("row", "col"), None, None),
        P(None, ("row", "col"), None),
    ) + (P(),) * 11
    out_specs = (P("row", None, "col", None, None), P(None, ("row", "col"), None))
    return jax.shard_map(shards, mesh=mesh, in_specs=in_specs, out_specs=out_specs, check_vma=False)
```

```python
import functools
import math

import jax
import jax.numpy as jnp
from jax import lax
from jax.experimental import pallas as pl
from jax.experimental.pallas import tpu as pltpu
from jax.sharding import PartitionSpec as P

epsilon = 1e-05
AXES = ("row", "col")
SUB = 8
LANES = 128
FLAT_ROWS = 1152
EXCLUDED = -1e30
SCALARS = pl.BlockSpec(memory_space=pltpu.SMEM)
BLOCK = pl.BlockSpec(memory_space=pltpu.VMEM)


def layer_norm(values, gain):
    mean = jnp.mean(values, axis=-1, keepdims=True)
    centered = values - mean
    variance = jnp.mean(centered * centered, axis=-1, keepdims=True)
    scaled = centered * lax.rsqrt(variance + epsilon)
    return scaled if gain is None else scaled * gain


def sigmoid(values):
    return 0.5 * jnp.tanh(0.5 * values) + 0.5


def gated(normed, weight):
    width = weight.shape[1] // 2
    hidden = jnp.dot(normed, weight, preferred_element_type=jnp.float32)
    return sigmoid(hidden[:, :width]) * hidden[:, width:]


def edge_rows(values, gain, weight):
    count, tokens, channels = values.shape
    flat = layer_norm(values.reshape(count * tokens, channels), gain).astype(jnp.bfloat16)
    return gated(flat, weight).reshape(count, tokens, channels)


def in_groups(rows, tokens, step):
    group = max(1, min(rows, FLAT_ROWS // tokens))
    while rows % group:
        group -= 1
    if group == rows:
        step(0, rows)
    else:
        lax.fori_loop(0, rows // group, lambda g, carry: (step(g * group, group), carry)[1], 0)


def right_kernel(place_ref, mask_ref, table_ref, gains_ref, weight_ref, *refs):
    pair_refs, right_ref = refs[:-1], refs[-1]
    rows, tokens, channels = pair_refs[0].shape
    gain = gains_ref[0:1]
    weight = weight_ref[:, 2 * channels : 4 * channels]
    row_index, col_index, col_count = place_ref[0], place_ref[1], place_ref[2]
    valid = jnp.broadcast_to((table_ref[0:1] == 1).astype(jnp.float32), (channels, tokens)).T
    for block, pair_ref in enumerate(pair_refs):
        first = ((row_index ^ block) * col_count + col_index) * rows

        def step(start, count):
            edges = edge_rows(pair_ref[pl.ds(start, count)].astype(jnp.float32), gain, weight)
            for i in range(count):
                own = (mask_ref[first + start + i] == 1).astype(jnp.float32)
                right_ref[block * rows + start + i] = (
                    (edges[i] * (valid * own)).astype(jnp.bfloat16).astype(jnp.float32)
                )

        in_groups(rows, tokens, step)


def pair_kernel(block_count, steps, head_count, place_ref, mask_ref, *refs):
    pair_refs = refs[: 2 * steps]
    right_ref, gains_ref, weight_ref, new_ref, head_ref, left_f, floats, tile_f, mixed_f = refs[
        2 * steps :
    ]
    rows, tokens, channels = pair_refs[0].shape
    pair_rows = 2 * rows
    gain, mix = gains_ref[0:1], gains_ref[1:2]
    weight = weight_ref[:, : 2 * channels]
    gate_weight = weight_ref[:, 4 * channels : 5 * channels]
    out_weight = weight_ref[:, 5 * channels : 6 * channels]
    bias_weight = weight_ref[:, 6 * channels : 6 * channels + head_count]
    row_index, col_index, col_count = place_ref[0], place_ref[1], place_ref[2]
    floats[:, tokens:] = jnp.zeros((rows, SUB, channels), jnp.float32)
    mixed_f[:, :, rows:, :] = jnp.zeros((pair_rows, block_count, SUB - rows, channels), jnp.float32)
    chip = col_index // 2
    for step_at in range(steps):
        for chunk, pair_ref in enumerate(pair_refs[2 * step_at : 2 * step_at + 2]):
            chunk_col = col_index ^ (2 * step_at + chunk)
            base = (chunk_col % 2) * rows
            first = (row_index * col_count + chunk_col) * rows

            def step(start, count):
                values = pair_ref[pl.ds(start, count)].astype(jnp.float32)
                floats[pl.ds(start, count), :tokens] = values
                edges = edge_rows(values, gain, weight)
                for i in range(count):
                    own = (mask_ref[first + start + i] == 1).astype(jnp.float32)
                    left_f[base + start + i] = (
                        (edges[i] * own).astype(jnp.bfloat16).astype(jnp.float32)
                    )

            in_groups(rows, tokens, step)
            for i in range(rows):
                for block in range(block_count):
                    start = ((row_index ^ block) * col_count + col_index) * rows
                    tile_f[base + i, block] = floats[i, pl.ds(start, SUB), :]

        def product(n, carry):
            block, half = n // 2, n % 2

            def slab(k, sums):
                at = pl.ds(pl.multiple_of(k * SUB, SUB), SUB)
                lefts = [left_f[half * rows + i, at, :] for i in range(rows)]
                rights = [right_ref[block * rows + t, at, :] for t in range(rows)]
                return tuple(
                    sums[i * rows + t] + lefts[i] * rights[t] for i in range(rows) for t in range(rows)
                )

            zero = jnp.zeros((SUB, channels), jnp.float32)
            sums = lax.fori_loop(0, tokens // SUB, slab, (zero,) * (rows * rows), unroll=24)
            for i in range(rows):
                for t in range(rows):
                    mixed_f[half * rows + i, block, t : t + 1, :] = jnp.sum(
                        sums[i * rows + t], axis=0, keepdims=True
                    )
            return carry

        lax.fori_loop(0, 2 * block_count, product, 0)
        flat = pair_rows * block_count * SUB
        mixed_norm = layer_norm(mixed_f[...].reshape(flat, channels), mix).astype(jnp.bfloat16)
        pair = tile_f[...].reshape(flat, channels)
        normed = layer_norm(pair, gain).astype(jnp.bfloat16)
        gate = sigmoid(jnp.dot(normed, gate_weight, preferred_element_type=jnp.float32))
        update = jnp.dot(mixed_norm, out_weight, preferred_element_type=jnp.float32)
        pair_new = (pair + gate * update).astype(jnp.bfloat16).astype(jnp.float32)
        split = pair_new.reshape(pair_rows, block_count, SUB, channels)
        bias_input = layer_norm(pair_new, None).astype(jnp.bfloat16)
        bias = lax.dot_general(
            bias_weight, bias_input, (((0,), (1,)), ((), ())), preferred_element_type=jnp.float32
        )
        place = chip ^ step_at
        for block in range(block_count):
            new_ref[pl.ds(place * pair_rows, pair_rows), row_index ^ block, 0] = split[
                :, block, :rows, :
            ].astype(jnp.bfloat16)
        head_ref[place] = bias.astype(jnp.bfloat16)


def project_kernel(block_count, place_ref, table_ref, weight_ref, *refs):
    single_refs = refs[:block_count]
    query_ref, key_ref, value_ref, allowed_ref, rows_f, own_f = refs[block_count:]
    col_count, rows, samples, width = single_refs[0].shape
    query_rows, key_count = allowed_ref.shape
    tokens = table_ref.shape[1]
    row_index, col_index = place_ref[0], place_ref[1]
    rows_f[...] = jnp.zeros_like(rows_f)
    own_f[...] = jnp.zeros_like(own_f)
    for col in range(col_count):
        for block in range(block_count):
            at = col * block_count + block
            for t in range(rows):
                values = single_refs[block][col_index ^ col, t].astype(jnp.float32)
                for s in range(samples):
                    rows_f[s, at, t : t + 1, :] = values[s : s + 1]
        for t in range(rows):
            values = single_refs[0][col, t].astype(jnp.float32)
            for s in range(samples):
                own_f[s, col, t : t + 1, :] = values[s : s + 1]
    for s in range(samples):
        own = own_f[s].reshape(-1, width).astype(jnp.bfloat16)
        query_ref[s] = jnp.dot(
            own, weight_ref[:, :width], preferred_element_type=jnp.float32
        ).astype(jnp.bfloat16)
        full = rows_f[s].reshape(-1, width).astype(jnp.bfloat16)
        for target, at in ((key_ref, width), (value_ref, 2 * width)):
            product = jnp.dot(
                full, weight_ref[:, at : at + width], preferred_element_type=jnp.float32
            )
            target[s] = product.T.astype(jnp.bfloat16)

    def key_tokens(shape, axis):
        place = lax.broadcasted_iota(jnp.int32, shape, axis)
        t = place % SUB
        block = (place // SUB) % block_count
        col = place // (SUB * block_count)
        token = ((row_index ^ block) * col_count + (col_index ^ col)) * rows + t
        return jnp.where(t < rows, token, -1)

    def query_tokens(shape):
        place = lax.broadcasted_iota(jnp.int32, shape, 0)
        t = place % SUB
        token = (row_index * col_count + place // SUB) * rows + t
        return jnp.where(t < rows, token, -2)

    chains = table_ref[1:2].astype(jnp.float32)
    valid = (table_ref[0:1] == 1).astype(jnp.float32)
    token = lax.broadcasted_iota(jnp.int32, (query_rows, tokens), 1)
    hit = query_tokens((query_rows, tokens)) == token
    query_chain = jnp.sum(jnp.where(hit, chains, 0.0), axis=1, keepdims=True)
    token = lax.broadcasted_iota(jnp.int32, (key_count, tokens), 1)
    hit = jnp.where(key_tokens((key_count, tokens), 0) == token, 1.0, 0.0).astype(jnp.bfloat16)

    def of_keys(table):
        table = jnp.broadcast_to(table, (SUB, tokens)).astype(jnp.bfloat16)
        return lax.dot_general(
            table, hit, (((1,), (1,)), ((), ())), preferred_element_type=jnp.float32
        )[:1]

    keys = key_tokens((query_rows, key_count), 1)
    near = (of_keys(valid) > 0.5) & (of_keys(chains) == query_chain) & (keys >= 0)
    allowed = near | (keys == query_tokens((query_rows, key_count)))
    allowed_ref[...] = jnp.where(allowed, 0.0, EXCLUDED)


def attend_kernel(col_count, token_rows, head_count, query_ref, key_ref, value_ref, *refs):
    bias_refs = refs[:col_count]
    allowed_ref, merge_ref, result_ref, bias_f, joined = refs[col_count:]
    samples, query_rows, width = query_ref.shape
    key_count = key_ref.shape[2]
    head_width = width // head_count
    scale = 1.0 / math.sqrt(head_width)
    part = key_count // col_count
    group = LANES // part
    pairs = bias_refs[0].shape[0]
    lane_tiles = bias_refs[0].shape[2] // LANES
    lane = lax.broadcasted_iota(jnp.int32, (head_count, LANES), 1) // part
    for col in range(col_count):
        for t in range(token_rows, SUB):
            bias_f[col * SUB + t] = jnp.zeros((head_count, key_count), jnp.float32)
    for pair in range(pairs):
        for tile in range(lane_tiles):
            pieces = [
                ref[pair, :, tile * LANES : (tile + 1) * LANES].astype(jnp.float32)
                for ref in bias_refs
            ]
            for m in range(group):
                inside = tile * group + m
                col = 2 * pair + inside // token_rows
                row = col * SUB + inside % token_rows
                for target in range(col_count // group):
                    total = None
                    for u in range(group):
                        piece = pieces[target * group + u]
                        shift = ((u - m) * part) % LANES
                        if shift:
                            piece = pltpu.roll(piece, shift, 1)
                        total = piece if total is None else jnp.where(lane == u, piece, total)
                    bias_f[row, :, target * LANES : (target + 1) * LANES] = total
    allowed = allowed_ref[...]
    parts = [[] for _ in range(samples)]
    for h in range(head_count):
        at = slice(h * head_width, (h + 1) * head_width)
        bias = bias_f[:, h, :] + allowed
        for s in range(samples):
            scores = jnp.dot(
                query_ref[s, :, at], key_ref[s, at, :], preferred_element_type=jnp.float32
            )
            scores = scores * scale + bias
            weights = jnp.exp(scores - jnp.max(scores, axis=-1, keepdims=True))
            weights = weights.astype(jnp.bfloat16)
            total = jnp.sum(weights.astype(jnp.float32), axis=-1, keepdims=True)
            summed = lax.dot_general(
                weights, value_ref[s, at, :], (((1,), (1,)), ((), ())),
                preferred_element_type=jnp.float32,
            )
            parts[s].append(summed / total)
    lane_parts = range(width // LANES)
    for s in range(samples):
        attended = jnp.concatenate(parts[s], axis=1)
        for n in lane_parts:
            joined[n, pl.ds(s, query_rows, stride=samples), :] = attended[
                :, n * LANES : (n + 1) * LANES
            ]
    attended = jnp.concatenate([joined[n] for n in lane_parts], axis=1).astype(jnp.bfloat16)
    merged = jnp.dot(attended, merge_ref[...], preferred_element_type=jnp.float32)
    split = merged.reshape(col_count, SUB * samples, width)
    result_ref[...] = split[:, : token_rows * samples, :].astype(jnp.bfloat16)


def call(kernel, name, operands, scalars, outs, scratch, time_us):
    def size(shape, kind):
        return math.prod(shape) * jnp.dtype(kind).itemsize

    held = sum(size(x.shape, x.dtype) for x in operands) + sum(size(*x) for x in outs)
    work = sum(size(*x) for x in scratch)
    limit = min(60 << 20, int(1.25 * (held + work)) + (6 << 20))
    return pl.pallas_call(
        kernel,
        in_specs=[SCALARS] * scalars + [BLOCK] * (len(operands) - scalars),
        out_specs=[BLOCK] * len(outs),
        out_shape=[jax.ShapeDtypeStruct(*x) for x in outs],
        scratch_shapes=[pltpu.VMEM(*x) for x in scratch],
        cost_estimate=pl.CostEstimate(
            flops=0, bytes_accessed=int(time_us * 3.6e6), transcendentals=0
        ),
        compiler_params=pltpu.CompilerParams(vmem_limit_bytes=limit),
        name=name,
    )(*operands)


def shards(
    pair_state,
    single_rep,
    token_mask,
    chain_ids,
    pair_gain,
    mix_gain,
    left_weight,
    right_weight,
    gate_weight,
    out_weight,
    bias_weight,
    token_weight,
    merge_weight,
):
    row_count = lax.axis_size("row")
    col_count = lax.axis_size("col")
    row_index = lax.axis_index("row")
    col_index = lax.axis_index("col")
    rows, tokens, channels = pair_state.shape
    samples, _, width = single_rep.shape
    heads = bias_weight.shape[1]
    chips = col_count // 2
    own_samples = samples // col_count
    keys = tokens // rows * SUB
    query_rows = col_count * SUB
    part = row_count * SUB
    bf16, f32 = jnp.bfloat16, jnp.float32

    def send(values, by_row, by_col):
        steps = [
            (r * col_count + c, (r ^ by_row) * col_count + (c ^ by_col))
            for r in range(row_count)
            for c in range(col_count)
        ]
        return lax.ppermute(values, AXES, steps)

    place = jnp.stack([row_index, col_index, jnp.int32(col_count)]).astype(jnp.int32)
    gains = jnp.stack([pair_gain, mix_gain])
    table = jnp.stack([token_mask, chain_ids])
    bias_columns = jnp.pad(bias_weight, ((0, 0), (0, LANES - heads)))
    weights = jnp.concatenate(
        [left_weight, right_weight, gate_weight, out_weight, bias_columns], axis=1
    )

    same = [pair_state] + [send(pair_state, 0, 2 * k) for k in range(1, chips)]
    other = [send(values, 0, 1) for values in same]
    columns = [pair_state] + [send(pair_state, k, 0) for k in range(1, row_count)]

    by_token = jnp.transpose(single_rep, (1, 0, 2)).reshape(rows, col_count, own_samples, width)
    own_single = lax.all_to_all(jnp.transpose(by_token, (1, 0, 2, 3)), "col", 0, 0, tiled=True)
    singles = [own_single] + [send(own_single, k, 0) for k in range(1, row_count)]

    (rights,) = call(
        right_kernel, "right_rows",
        [place, token_mask, table, gains, weights, *columns], 2,
        [((row_count * rows, tokens, channels), f32)], [], 3.0,
    )
    pair_new, pair_heads = call(
        functools.partial(pair_kernel, row_count, chips, heads), "pair_rows",
        [
            place, token_mask, *(x for k in range(chips) for x in (same[k], other[k])), rights,
            gains, weights,
        ], 2,
        [
            ((rows * col_count, row_count, 1, rows, channels), bf16),
            ((chips, heads, 2 * rows * part), bf16),
        ],
        [
            ((2 * rows, tokens, channels), f32),
            ((rows, tokens + SUB, channels), f32),
            ((2 * rows, row_count, SUB, channels), f32),
            ((2 * rows, row_count, SUB, channels), f32),
        ], 4.0,
    )

    queries, key_cols, value_cols, allowed = call(
        functools.partial(project_kernel, row_count), "project_tokens",
        [place, table, token_weight, *singles], 1,
        [
            ((own_samples, query_rows, width), bf16),
            ((own_samples, width, keys), bf16),
            ((own_samples, width, keys), bf16),
            ((query_rows, keys), f32),
        ],
        [
            ((own_samples, keys // SUB, SUB, width), f32),
            ((own_samples, col_count, SUB, width), f32),
        ], 5.0,
    )

    near = [pair_heads] + [send(pair_heads, 0, 2 * k) for k in range(1, chips)]
    near, allowed = lax.optimization_barrier((near, allowed))
    biases = []
    for values in near:
        biases += [values, send(values, 0, 1)]

    (merged,) = call(
        functools.partial(attend_kernel, col_count, rows, heads), "attend",
        [queries, key_cols, value_cols, *biases, allowed, merge_weight], 0,
        [((col_count, rows * own_samples, width), bf16)],
        [((query_rows, heads, keys), f32), ((width // LANES, own_samples * query_rows, LANES), f32)], 6.0,
    )
    arrived = lax.all_to_all(merged, "col", 0, 0, tiled=True)
    arrived = arrived.reshape(col_count, rows, own_samples, width)
    attention_out = jnp.transpose(arrived, (0, 2, 1, 3)).reshape(samples, rows, width)
    return pair_new, attention_out


def solution(mesh):
    in_specs = (
        P(("row", "col"), None, None),
        P(None, ("row", "col"), None),
    ) + (P(),) * 11
    out_specs = (P("row", None, "col", None, None), P(None, ("row", "col"), None))
    return jax.shard_map(shards, mesh=mesh, in_specs=in_specs, out_specs=out_specs, check_vma=False)
```

```python
import functools
import math

import jax
import jax.numpy as jnp
from jax import lax
from jax.experimental import pallas as pl
from jax.experimental.pallas import tpu as pltpu
from jax.sharding import PartitionSpec as P

epsilon = 1e-05
AXES = ("row", "col")
SUB = 8
LANES = 128
FLAT_ROWS = 1152
EXCLUDED = -1e30
SCALARS = pl.BlockSpec(memory_space=pltpu.SMEM)
BLOCK = pl.BlockSpec(memory_space=pltpu.VMEM)


def layer_norm(values, gain):
    mean = jnp.mean(values, axis=-1, keepdims=True)
    centered = values - mean
    variance = jnp.mean(centered * centered, axis=-1, keepdims=True)
    scaled = centered * lax.rsqrt(variance + epsilon)
    return scaled if gain is None else scaled * gain


def sigmoid(values):
    return 0.5 * jnp.tanh(0.5 * values) + 0.5


def gated(normed, weight):
    width = weight.shape[1] // 2
    hidden = jnp.dot(normed, weight, preferred_element_type=jnp.float32)
    return sigmoid(hidden[:, :width]) * hidden[:, width:]


def edge_rows(values, gain, weight):
    count, tokens, channels = values.shape
    flat = layer_norm(values.reshape(count * tokens, channels), gain).astype(jnp.bfloat16)
    return gated(flat, weight).reshape(count, tokens, channels)


def in_groups(rows, tokens, step):
    group = max(1, min(rows, FLAT_ROWS // tokens))
    while rows % group:
        group -= 1
    if group == rows:
        step(0, rows)
    else:
        lax.fori_loop(0, rows // group, lambda g, carry: (step(g * group, group), carry)[1], 0)


def right_kernel(place_ref, mask_ref, table_ref, gains_ref, weight_ref, *refs):
    pair_refs, right_ref = refs[:-1], refs[-1]
    rows, tokens, channels = pair_refs[0].shape
    gain = gains_ref[0:1]
    weight = weight_ref[:, 2 * channels : 4 * channels]
    row_index, col_index, col_count = place_ref[0], place_ref[1], place_ref[2]
    valid = jnp.broadcast_to((table_ref[0:1] == 1).astype(jnp.float32), (channels, tokens)).T
    for block, pair_ref in enumerate(pair_refs):
        first = ((row_index ^ block) * col_count + col_index) * rows

        def step(start, count):
            edges = edge_rows(pair_ref[pl.ds(start, count)].astype(jnp.float32), gain, weight)
            for i in range(count):
                own = (mask_ref[first + start + i] == 1).astype(jnp.float32)
                right_ref[block * rows + start + i] = (
                    (edges[i] * (valid * own)).astype(jnp.bfloat16).astype(jnp.float32)
                )

        in_groups(rows, tokens, step)


def pair_kernel(block_count, steps, head_count, place_ref, mask_ref, *refs):
    pair_refs = refs[: 2 * steps]
    right_ref, gains_ref, weight_ref, new_ref, head_ref, left_f, floats, tile_f, mixed_f = refs[
        2 * steps :
    ]
    rows, tokens, channels = pair_refs[0].shape
    pair_rows = 2 * rows
    gain, mix = gains_ref[0:1], gains_ref[1:2]
    weight = weight_ref[:, : 2 * channels]
    gate_weight = weight_ref[:, 4 * channels : 5 * channels]
    out_weight = weight_ref[:, 5 * channels : 6 * channels]
    bias_weight = weight_ref[:, 6 * channels : 6 * channels + head_count]
    row_index, col_index, col_count = place_ref[0], place_ref[1], place_ref[2]
    floats[:, tokens:] = jnp.zeros((rows, SUB, channels), jnp.float32)
    mixed_f[:, :, rows:, :] = jnp.zeros((pair_rows, block_count, SUB - rows, channels), jnp.float32)
    chip = col_index // 2
    for step_at in range(steps):
        for chunk, pair_ref in enumerate(pair_refs[2 * step_at : 2 * step_at + 2]):
            chunk_col = col_index ^ (2 * step_at + chunk)
            base = (chunk_col % 2) * rows
            first = (row_index * col_count + chunk_col) * rows

            def step(start, count):
                values = pair_ref[pl.ds(start, count)].astype(jnp.float32)
                floats[pl.ds(start, count), :tokens] = values
                edges = edge_rows(values, gain, weight)
                for i in range(count):
                    own = (mask_ref[first + start + i] == 1).astype(jnp.float32)
                    left_f[base + start + i] = (
                        (edges[i] * own).astype(jnp.bfloat16).astype(jnp.float32)
                    )

            in_groups(rows, tokens, step)
            for i in range(rows):
                for block in range(block_count):
                    start = ((row_index ^ block) * col_count + col_index) * rows
                    tile_f[base + i, block] = floats[i, pl.ds(start, SUB), :]

        def product(n, carry):
            block, half = n // 2, n % 2

            def slab(k, sums):
                at = pl.ds(pl.multiple_of(k * SUB, SUB), SUB)
                lefts = [left_f[half * rows + i, at, :] for i in range(rows)]
                rights = [right_ref[block * rows + t, at, :] for t in range(rows)]
                return tuple(
                    sums[i * rows + t] + lefts[i] * rights[t] for i in range(rows) for t in range(rows)
                )

            zero = jnp.zeros((SUB, channels), jnp.float32)
            sums = lax.fori_loop(0, tokens // SUB, slab, (zero,) * (rows * rows), unroll=24)
            for i in range(rows):
                for t in range(rows):
                    mixed_f[half * rows + i, block, t : t + 1, :] = jnp.sum(
                        sums[i * rows + t], axis=0, keepdims=True
                    )
            return carry

        lax.fori_loop(0, 2 * block_count, product, 0, unroll=2)
        flat = pair_rows * block_count * SUB
        mixed_norm = layer_norm(mixed_f[...].reshape(flat, channels), mix).astype(jnp.bfloat16)
        pair = tile_f[...].reshape(flat, channels)
        normed = layer_norm(pair, gain).astype(jnp.bfloat16)
        gate = sigmoid(jnp.dot(normed, gate_weight, preferred_element_type=jnp.float32))
        update = jnp.dot(mixed_norm, out_weight, preferred_element_type=jnp.float32)
        pair_new = (pair + gate * update).astype(jnp.bfloat16).astype(jnp.float32)
        split = pair_new.reshape(pair_rows, block_count, SUB, channels)
        bias_input = layer_norm(pair_new, None).astype(jnp.bfloat16)
        bias = lax.dot_general(
            bias_weight, bias_input, (((0,), (1,)), ((), ())), preferred_element_type=jnp.float32
        )
        place = chip ^ step_at
        for block in range(block_count):
            new_ref[pl.ds(place * pair_rows, pair_rows), row_index ^ block, 0] = split[
                :, block, :rows, :
            ].astype(jnp.bfloat16)
        head_ref[place] = bias.astype(jnp.bfloat16)


def project_kernel(block_count, place_ref, table_ref, weight_ref, *refs):
    single_refs = refs[:block_count]
    query_ref, key_ref, value_ref, allowed_ref, rows_f, own_f = refs[block_count:]
    col_count, rows, samples, width = single_refs[0].shape
    query_rows, key_count = allowed_ref.shape
    tokens = table_ref.shape[1]
    row_index, col_index = place_ref[0], place_ref[1]
    rows_f[...] = jnp.zeros_like(rows_f)
    own_f[...] = jnp.zeros_like(own_f)
    for col in range(col_count):
        for block in range(block_count):
            at = col * block_count + block
            for t in range(rows):
                values = single_refs[block][col_index ^ col, t].astype(jnp.float32)
                for s in range(samples):
                    rows_f[s, at, t : t + 1, :] = values[s : s + 1]
        for t in range(rows):
            values = single_refs[0][col, t].astype(jnp.float32)
            for s in range(samples):
                own_f[s, col, t : t + 1, :] = values[s : s + 1]
    for s in range(samples):
        own = own_f[s].reshape(-1, width).astype(jnp.bfloat16)
        query_ref[s] = jnp.dot(
            own, weight_ref[:, :width], preferred_element_type=jnp.float32
        ).astype(jnp.bfloat16)
        full = rows_f[s].reshape(-1, width).astype(jnp.bfloat16)
        for target, at in ((key_ref, width), (value_ref, 2 * width)):
            product = jnp.dot(
                full, weight_ref[:, at : at + width], preferred_element_type=jnp.float32
            )
            target[s] = product.T.astype(jnp.bfloat16)

    def key_tokens(shape, axis):
        place = lax.broadcasted_iota(jnp.int32, shape, axis)
        t = place % SUB
        block = (place // SUB) % block_count
        col = place // (SUB * block_count)
        token = ((row_index ^ block) * col_count + (col_index ^ col)) * rows + t
        return jnp.where(t < rows, token, -1)

    def query_tokens(shape):
        place = lax.broadcasted_iota(jnp.int32, shape, 0)
        t = place % SUB
        token = (row_index * col_count + place // SUB) * rows + t
        return jnp.where(t < rows, token, -2)

    chains = table_ref[1:2].astype(jnp.float32)
    valid = (table_ref[0:1] == 1).astype(jnp.float32)
    token = lax.broadcasted_iota(jnp.int32, (query_rows, tokens), 1)
    hit = query_tokens((query_rows, tokens)) == token
    query_chain = jnp.sum(jnp.where(hit, chains, 0.0), axis=1, keepdims=True)
    token = lax.broadcasted_iota(jnp.int32, (key_count, tokens), 1)
    hit = jnp.where(key_tokens((key_count, tokens), 0) == token, 1.0, 0.0).astype(jnp.bfloat16)

    def of_keys(table):
        table = jnp.broadcast_to(table, (SUB, tokens)).astype(jnp.bfloat16)
        return lax.dot_general(
            table, hit, (((1,), (1,)), ((), ())), preferred_element_type=jnp.float32
        )[:1]

    keys = key_tokens((query_rows, key_count), 1)
    near = (of_keys(valid) > 0.5) & (of_keys(chains) == query_chain) & (keys >= 0)
    allowed = near | (keys == query_tokens((query_rows, key_count)))
    allowed_ref[...] = jnp.where(allowed, 0.0, EXCLUDED)


def attend_kernel(col_count, token_rows, head_count, query_ref, key_ref, value_ref, *refs):
    bias_refs = refs[:col_count]
    allowed_ref, merge_ref, result_ref, bias_f, joined = refs[col_count:]
    samples, query_rows, width = query_ref.shape
    key_count = key_ref.shape[2]
    head_width = width // head_count
    scale = 1.0 / math.sqrt(head_width)
    part = key_count // col_count
    group = LANES // part
    pairs = bias_refs[0].shape[0]
    lane_tiles = bias_refs[0].shape[2] // LANES
    lane = lax.broadcasted_iota(jnp.int32, (head_count, LANES), 1) // part
    for col in range(col_count):
        for t in range(token_rows, SUB):
            bias_f[col * SUB + t] = jnp.zeros((head_count, key_count), jnp.float32)
    for pair in range(pairs):
        for tile in range(lane_tiles):
            pieces = [
                ref[pair, :, tile * LANES : (tile + 1) * LANES].astype(jnp.float32)
                for ref in bias_refs
            ]
            for m in range(group):
                inside = tile * group + m
                col = 2 * pair + inside // token_rows
                row = col * SUB + inside % token_rows
                for target in range(col_count // group):
                    total = None
                    for u in range(group):
                        piece = pieces[target * group + u]
                        shift = ((u - m) * part) % LANES
                        if shift:
                            piece = pltpu.roll(piece, shift, 1)
                        total = piece if total is None else jnp.where(lane == u, piece, total)
                    bias_f[row, :, target * LANES : (target + 1) * LANES] = total
    allowed = allowed_ref[...]
    parts = [[] for _ in range(samples)]
    for h in range(head_count):
        at = slice(h * head_width, (h + 1) * head_width)
        bias = bias_f[:, h, :] + allowed
        for s in range(samples):
            scores = jnp.dot(
                query_ref[s, :, at], key_ref[s, at, :], preferred_element_type=jnp.float32
            )
            scores = scores * scale + bias
            weights = jnp.exp(scores - jnp.max(scores, axis=-1, keepdims=True))
            weights = weights.astype(jnp.bfloat16)
            total = jnp.sum(weights.astype(jnp.float32), axis=-1, keepdims=True)
            summed = lax.dot_general(
                weights, value_ref[s, at, :], (((1,), (1,)), ((), ())),
                preferred_element_type=jnp.float32,
            )
            parts[s].append(summed / total)
    lane_parts = range(width // LANES)
    for s in range(samples):
        attended = jnp.concatenate(parts[s], axis=1)
        for n in lane_parts:
            joined[n, pl.ds(s, query_rows, stride=samples), :] = attended[
                :, n * LANES : (n + 1) * LANES
            ]
    attended = jnp.concatenate([joined[n] for n in lane_parts], axis=1).astype(jnp.bfloat16)
    merged = jnp.dot(attended, merge_ref[...], preferred_element_type=jnp.float32)
    split = merged.reshape(col_count, SUB * samples, width)
    result_ref[...] = split[:, : token_rows * samples, :].astype(jnp.bfloat16)


def call(kernel, name, operands, scalars, outs, scratch, time_us):
    def size(shape, kind):
        return math.prod(shape) * jnp.dtype(kind).itemsize

    held = sum(size(x.shape, x.dtype) for x in operands) + sum(size(*x) for x in outs)
    work = sum(size(*x) for x in scratch)
    limit = min(60 << 20, int(1.25 * (held + work)) + (6 << 20))
    return pl.pallas_call(
        kernel,
        in_specs=[SCALARS] * scalars + [BLOCK] * (len(operands) - scalars),
        out_specs=[BLOCK] * len(outs),
        out_shape=[jax.ShapeDtypeStruct(*x) for x in outs],
        scratch_shapes=[pltpu.VMEM(*x) for x in scratch],
        cost_estimate=pl.CostEstimate(
            flops=0, bytes_accessed=int(time_us * 3.6e6), transcendentals=0
        ),
        compiler_params=pltpu.CompilerParams(vmem_limit_bytes=limit),
        name=name,
    )(*operands)


def shards(
    pair_state,
    single_rep,
    token_mask,
    chain_ids,
    pair_gain,
    mix_gain,
    left_weight,
    right_weight,
    gate_weight,
    out_weight,
    bias_weight,
    token_weight,
    merge_weight,
):
    row_count = lax.axis_size("row")
    col_count = lax.axis_size("col")
    row_index = lax.axis_index("row")
    col_index = lax.axis_index("col")
    rows, tokens, channels = pair_state.shape
    samples, _, width = single_rep.shape
    heads = bias_weight.shape[1]
    chips = col_count // 2
    own_samples = samples // col_count
    keys = tokens // rows * SUB
    query_rows = col_count * SUB
    part = row_count * SUB
    bf16, f32 = jnp.bfloat16, jnp.float32

    def send(values, by_row, by_col):
        steps = [
            (r * col_count + c, (r ^ by_row) * col_count + (c ^ by_col))
            for r in range(row_count)
            for c in range(col_count)
        ]
        return lax.ppermute(values, AXES, steps)

    place = jnp.stack([row_index, col_index, jnp.int32(col_count)]).astype(jnp.int32)
    gains = jnp.stack([pair_gain, mix_gain])
    table = jnp.stack([token_mask, chain_ids])
    bias_columns = jnp.pad(bias_weight, ((0, 0), (0, LANES - heads)))
    weights = jnp.concatenate(
        [left_weight, right_weight, gate_weight, out_weight, bias_columns], axis=1
    )

    same = [pair_state] + [send(pair_state, 0, 2 * k) for k in range(1, chips)]
    other = [send(values, 0, 1) for values in same]
    columns = [pair_state] + [send(pair_state, k, 0) for k in range(1, row_count)]

    by_token = jnp.transpose(single_rep, (1, 0, 2)).reshape(rows, col_count, own_samples, width)
    own_single = lax.all_to_all(jnp.transpose(by_token, (1, 0, 2, 3)), "col", 0, 0, tiled=True)
    singles = [own_single] + [send(own_single, k, 0) for k in range(1, row_count)]

    (rights,) = call(
        right_kernel, "right_rows",
        [place, token_mask, table, gains, weights, *columns], 2,
        [((row_count * rows, tokens, channels), f32)], [], 3.0,
    )
    pair_new, pair_heads = call(
        functools.partial(pair_kernel, row_count, chips, heads), "pair_rows",
        [
            place, token_mask, *(x for k in range(chips) for x in (same[k], other[k])), rights,
            gains, weights,
        ], 2,
        [
            ((rows * col_count, row_count, 1, rows, channels), bf16),
            ((chips, heads, 2 * rows * part), bf16),
        ],
        [
            ((2 * rows, tokens, channels), f32),
            ((rows, tokens + SUB, channels), f32),
            ((2 * rows, row_count, SUB, channels), f32),
            ((2 * rows, row_count, SUB, channels), f32),
        ], 4.0,
    )

    queries, key_cols, value_cols, allowed = call(
        functools.partial(project_kernel, row_count), "project_tokens",
        [place, table, token_weight, *singles], 1,
        [
            ((own_samples, query_rows, width), bf16),
            ((own_samples, width, keys), bf16),
            ((own_samples, width, keys), bf16),
            ((query_rows, keys), f32),
        ],
        [
            ((own_samples, keys // SUB, SUB, width), f32),
            ((own_samples, col_count, SUB, width), f32),
        ], 5.0,
    )

    near = [pair_heads] + [send(pair_heads, 0, 2 * k) for k in range(1, chips)]
    near, allowed = lax.optimization_barrier((near, allowed))
    biases = []
    for values in near:
        biases += [values, send(values, 0, 1)]

    (merged,) = call(
        functools.partial(attend_kernel, col_count, rows, heads), "attend",
        [queries, key_cols, value_cols, *biases, allowed, merge_weight], 0,
        [((col_count, rows * own_samples, width), bf16)],
        [((query_rows, heads, keys), f32), ((width // LANES, own_samples * query_rows, LANES), f32)], 6.0,
    )
    arrived = lax.all_to_all(merged, "col", 0, 0, tiled=True)
    arrived = arrived.reshape(col_count, rows, own_samples, width)
    attention_out = jnp.transpose(arrived, (0, 2, 1, 3)).reshape(samples, rows, width)
    return pair_new, attention_out


def solution(mesh):
    in_specs = (
        P(("row", "col"), None, None),
        P(None, ("row", "col"), None),
    ) + (P(),) * 11
    out_specs = (P("row", None, "col", None, None), P(None, ("row", "col"), None))
    return jax.shard_map(shards, mesh=mesh, in_specs=in_specs, out_specs=out_specs, check_vma=False)
```
